512 devices in a mesh: replica: 32 (over z, core), tensor: 16 (over y, x).
Axes of the slice: x: 4, y: 4, z: 16, core: 2. Of those that a mesh axis runs over, the one named last changes fastest.
Arguments:
- tokens: bfloat16 [24576, 4096], P('replica', 'tensor'), may hold values from -6 to 6
- query_weight: bfloat16 [4096, 4096], P(None, 'tensor'), may hold values from -0.09375 to 0.09375
- input_factor_pool: bfloat16 [1024, 64, 4096], P('replica', None, 'tensor'), may hold values from -0.09375 to 0.09375
- output_factor_pool: bfloat16 [1024, 64, 4096], P('replica', None, 'tensor'), may hold values from -0.375 to 0.375
- row_adapter_index: int32 [24576], P('replica'), may hold values from 0 to 1023, as said below
- adapter_pool_slot: int32 [1024], replicated, may hold values from 0 to 1023, as said below
Outputs:
- queries: bfloat16 [24576, 4096], P('replica', 'tensor')
The draws below stay inside these ranges and needn't reach their ends.
Inputs may be any that keep to these rules, and one draw needn't show every extreme that they name: Each of 0 to 1023 appears once; adapter a uses entry adapter_pool_slot[a] of the first dimension of input_factor_pool and output_factor_pool, and its holder is adapter_pool_slot[a] // 32. `row_adapter_index`: among the 768 rows of one group (one index of replica), at most 16 rows name any one adapter, and at most 4 different named adapters share one holder. In every group some adapter is named by exactly 16 rows and some holder has exactly 4 named adapters.
All inputs are finite; a program needn't handle non-finite values.
Results may differ from the reference program's by a relative error of at most 0.0049.
Values may be sent and summed in bfloat16 or wider, within the bound.
No kernel may reach another device: no remote copies, remote signals or barrier semaphores. Data moves between devices by JAX's collectives and lax.ppermute only.
A program may use at most 64 MiB of HBM per device.

```python
import jax
import jax.numpy as jnp
from jax import lax

INPUT_WIDTH = 4096
ADAPTER_RANK = 64
ROWS = 768
ADP_REP = 32
DISTINCT = 128
RPA = 16
QUERY_COLUMNS = 4096
ADAPTER_COUNT = 1024
ROWS_ALL = 24576
N_REPLICA = 32


def pool_order(key):
    return jax.random.permutation(jax.random.fold_in(key, 101), ADAPTER_COUNT).astype(jnp.int32)


def draw_adapter_pool_slot(key, part):
    shared = pool_order(key)
    return shared


def draw_row_adapter_index(key, part):
    slot_of = pool_order(key)
    key = jax.random.fold_in(key, 5)
    adapter_of_slot = jnp.argsort(slot_of, stable=True).astype(jnp.int32)
    caps = DISTINCT // N_REPLICA
    width = N_REPLICA * caps * RPA
    hot_count = max(N_REPLICA // 4, 1)

    def one_group(group_key):
        keys = jax.random.split(group_key, 5)
        local_sets = jax.vmap(lambda inner: jax.random.permutation(inner, ADP_REP)[:caps])(jax.random.split(keys[0], N_REPLICA))
        hot_flag = jax.random.permutation(keys[1], N_REPLICA) < hot_count
        focus = jax.random.randint(keys[2], (), 0, N_REPLICA)
        position = jnp.arange(width, dtype=jnp.int32)
        holder_at = position // (caps * RPA)
        column_at = position // RPA % caps
        depth_at = position % RPA
        forced = (holder_at == focus) & ((column_at == 0) | (depth_at == 0))
        score = jax.random.randint(keys[3], (width,), 0, 4096)
        score = score + jnp.where(hot_flag[holder_at], 4096, 0) + jnp.where(forced, 8192, 0)
        score = score * width + position
        top_scores, chosen = lax.top_k(score, ROWS)
        slots = holder_at[chosen] * ADP_REP + local_sets[holder_at[chosen], column_at[chosen]]
        shuffle = jax.random.permutation(keys[4], ROWS)
        return adapter_of_slot[slots[shuffle]]
    group_count = jax.vmap(one_group)(jax.random.split(key, N_REPLICA))
    return group_count.reshape(-1).astype(jnp.int32)


def block_levels(rng, extent, cuts, smallest, high):
    loudness, own = 1.0, jax.random.fold_in(rng, 6)
    for dim, blocks in cuts:
        draws = jnp.exp(jax.random.uniform(jax.random.fold_in(own, dim), (blocks,), jnp.float32, smallest / len(cuts), high / len(cuts)))
        loudness = loudness * jnp.repeat(draws, extent[dim] // blocks).reshape([-1 if axis == dim else 1 for axis in range(len(extent))])
    return loudness


def bell_draw(rng, dims, scale, bound, pieces=(), held_as=jnp.bfloat16):
    factor_of = block_levels(rng, dims, pieces, -0.22, 0.18) if pieces else 1.0
    values = jax.random.normal(rng, dims, jnp.float32) * scale * factor_of
    return jnp.minimum(jnp.maximum(values, -bound), bound).astype(held_as)


def setup_inputs(seed: int = 0) -> dict:
    seeds = jax.random.split(jax.random.key(seed), 7)
    return {
        "tokens": bell_draw(seeds[0], (ROWS_ALL, INPUT_WIDTH), 1.0, 6.0, ((0, 32), (1, 16))),
        "query_weight": bell_draw(seeds[1], (INPUT_WIDTH, QUERY_COLUMNS), INPUT_WIDTH ** -0.5, 0.09375, ((1, 16),)),
        "input_factor_pool": bell_draw(seeds[2], (ADAPTER_COUNT, ADAPTER_RANK, INPUT_WIDTH), INPUT_WIDTH ** -0.5, 0.09375, ((0, 32), (2, 16))),
        "output_factor_pool": bell_draw(seeds[3], (ADAPTER_COUNT, ADAPTER_RANK, QUERY_COLUMNS), (4 * ADAPTER_RANK) ** -0.5, 0.375, ((0, 32), (2, 16))),
        "row_adapter_index": draw_row_adapter_index(jax.random.fold_in(seeds[6], 71), 0),
        "adapter_pool_slot": draw_adapter_pool_slot(jax.random.fold_in(seeds[6], 71), 0),
    }


adapter_scale = 2.0


def reference(tokens, query_weight, input_factor_pool, output_factor_pool, row_adapter_index, adapter_pool_slot):
    pool_row = adapter_pool_slot[row_adapter_index].astype(jnp.int32)
    base_output = jnp.dot(tokens, query_weight, preferred_element_type=jnp.float32)

    def per_block(pair):
        token_block, pool_slot_block = pair
        adapter_input_factor = input_factor_pool[pool_slot_block].astype(jnp.float32)
        adapter_output_factor = output_factor_pool[pool_slot_block].astype(jnp.float32)
        shrunk = jnp.einsum("nf,nkf->nk", token_block.astype(jnp.float32), adapter_input_factor).astype(jnp.bfloat16)
        shrunk = lax.optimization_barrier(shrunk)
        expanded_rows = jnp.einsum("nk,nkc->nc", shrunk.astype(jnp.float32), adapter_output_factor)
        return expanded_rows.astype(jnp.bfloat16)

    expanded_rows = lax.map(per_block, (tokens.reshape(-1, 32, INPUT_WIDTH), pool_row.reshape(-1, 32)))
    expanded_rows = lax.optimization_barrier(expanded_rows.reshape(ROWS_ALL, QUERY_COLUMNS))
    return (base_output + adapter_scale * expanded_rows.astype(jnp.float32)).astype(jnp.bfloat16)
```

```python
import jax
import jax.numpy as jnp
from jax import lax
from jax.experimental import pallas as pl
from jax.experimental.pallas import tpu as pltpu
from jax.sharding import PartitionSpec as P

RANK = 64
SLOTS = 4
RPA = 16
PAIR = SLOTS * RPA
GROUPS = 32
HELD = 32
TENSOR = 16
ROWS = 768
WIDTH = 256
BUCKETS = GROUPS * PAIR
PAY = 136
SCALE = 2.0

BF = jnp.bfloat16
F32 = jnp.float32
I32 = jnp.int32
NT = (((1,), (1,)), ((), ()))


def params():
    return pltpu.CompilerParams(vmem_limit_bytes=40 * 1024 * 1024)


def vmem(n):
    return [pl.BlockSpec(memory_space=pltpu.VMEM)] * n


def pack_kernel(dest_ref, local_ref, tokens_ref, out_ref):
    dest = dest_ref[...]
    local = local_ref[...]
    for b in range(8):
        at = lax.broadcasted_iota(I32, (256, ROWS), 0) + b * 256
        pick = (at == dest).astype(F32).astype(BF)
        rows = jnp.dot(pick, tokens_ref[...], preferred_element_type=F32).astype(BF)
        for j in range(4):
            out_ref[4 * b + j, 0:64, :] = rows[64 * j : 64 * j + 64, 0:128]
            out_ref[4 * b + j, 64:128, :] = rows[64 * j : 64 * j + 64, 128:256]
    group = lax.broadcasted_iota(I32, (GROUPS, ROWS), 0)
    to = (group == dest // PAIR).astype(F32).astype(BF)
    lane_slot = (lax.broadcasted_iota(I32, (128, ROWS), 0) % PAIR) // RPA
    slot = (dest % PAIR) // RPA
    first = dest % RPA == 0
    value = jnp.where((lane_slot == slot) & first, local.astype(F32), 0.0).astype(BF)
    ids = lax.dot_general(to, value, NT, preferred_element_type=F32).astype(BF)
    for h in range(GROUPS):
        out_ref[h, 128:136, :] = jnp.broadcast_to(ids[h : h + 1, :], (8, 128))


def shrink_kernel(pay_ref, a_ref, out_ref, ids_ref):
    low = lax.broadcasted_iota(I32, (8, 128), 1) < PAIR
    for b in range(8):
        parts = []
        marks = []
        for j in range(4):
            g = 4 * b + j
            parts.append(jnp.concatenate([pay_ref[g, 0:64, :], pay_ref[g, 64:128, :]], axis=1))
        for j in range(2):
            g = 4 * b + 2 * j
            mark = jnp.where(
                low, pay_ref[g, 128:136, :].astype(F32), pay_ref[g + 1, 128:136, :].astype(F32)
            ).astype(I32)
            ids_ref[2 * b + j] = mark
            marks.append(mark[0:1, :])
        rows = jnp.concatenate(parts, axis=0)
        mark = jnp.concatenate(marks, axis=1)
        total = jnp.zeros((RANK, 256), F32)
        for q in range(8):
            prod = lax.dot_general(
                a_ref[256 * q : 256 * q + 256, :], rows, NT, preferred_element_type=F32
            )
            for a in range(4):
                total = total + jnp.where(mark == 4 * q + a, prod[64 * a : 64 * a + 64], 0.0)
        out_ref[2 * b] = total[:, 0:128].astype(BF)
        out_ref[2 * b + 1] = total[:, 128:256].astype(BF)


def sum_kernel(p_ref, out_ref):
    total = p_ref[0].astype(F32)
    for t in range(1, TENSOR):
        total = total + p_ref[t].astype(F32)
    mine = total.astype(BF)
    for t in range(TENSOR):
        out_ref[t] = mine


def expand_kernel(s_ref, ids_ref, bt_ref, out_ref, m_ref):
    for b in range(8):
        s = jnp.concatenate([s_ref[2 * b], s_ref[2 * b + 1]], axis=1).astype(F32)
        mark = jnp.concatenate([ids_ref[2 * b][0:1], ids_ref[2 * b + 1][0:1]], axis=1)
        for a in range(HELD):
            m_ref[64 * a : 64 * a + 64, :] = jnp.where(mark == a, s, 0.0).astype(BF)
        et = jnp.dot(bt_ref[...], m_ref[...], preferred_element_type=F32)
        rows = et.T.astype(BF)
        for j in range(4):
            out_ref[4 * b + j] = rows[64 * j : 64 * j + 64]


def final_kernel(dest_ref, base_ref, back_ref, out_ref):
    for b in range(3):
        at = lax.broadcasted_iota(I32, (256, BUCKETS), 1)
        pick = (at == dest_ref[256 * b : 256 * b + 256, :]).astype(F32).astype(BF)
        rows = jnp.dot(pick, back_ref[...], preferred_element_type=F32)
        out_ref[256 * b : 256 * b + 256, :] = (
            base_ref[256 * b : 256 * b + 256, :] + SCALE * rows
        ).astype(BF)


def route(row_adapter_index, adapter_pool_slot):
    table_ids = jnp.arange(adapter_pool_slot.shape[0], dtype=I32)
    pool_row = jnp.sum(
        jnp.where(row_adapter_index[:, None] == table_ids[None, :], adapter_pool_slot[None, :], 0),
        axis=1,
    )
    holder = pool_row // HELD
    order = jnp.arange(ROWS, dtype=I32)
    same = pool_row[:, None] == pool_row[None, :]
    place = jnp.sum(same & (order[None, :] < order[:, None]), axis=1)
    first = place == 0
    same_holder = holder[:, None] == holder[None, :]
    rank = jnp.sum(
        first[None, :] & same_holder & (pool_row[None, :] < pool_row[:, None]), axis=1
    )
    return (holder * SLOTS + rank) * RPA + place, pool_row % HELD


def exchange(x, axis):
    return lax.all_to_all(x, axis, split_axis=0, concat_axis=0, tiled=True)


def body(tokens, weight, a_pool, b_pool, row_adapter_index, adapter_pool_slot):
    everything = lax.all_gather(tokens, "tensor", axis=1, tiled=True)
    dest, local = route(row_adapter_index, adapter_pool_slot)
    payload = pl.pallas_call(
        pack_kernel,
        out_shape=jax.ShapeDtypeStruct((GROUPS, PAY, 128), BF),
        in_specs=vmem(3),
        out_specs=pl.BlockSpec(memory_space=pltpu.VMEM),
        compiler_params=params(),
        name="pack",
    )(dest.reshape(1, ROWS), local.reshape(1, ROWS), tokens)
    arrived = exchange(payload, "replica")
    partial, ids = pl.pallas_call(
        shrink_kernel,
        out_shape=(
            jax.ShapeDtypeStruct((TENSOR, RANK, 128), BF),
            jax.ShapeDtypeStruct((TENSOR, 8, 128), I32),
        ),
        in_specs=vmem(2),
        out_specs=tuple(vmem(2)),
        compiler_params=params(),
        name="shrink",
    )(arrived, a_pool.reshape(HELD * RANK, WIDTH))
    summed = pl.pallas_call(
        sum_kernel,
        out_shape=jax.ShapeDtypeStruct((TENSOR, RANK, 128), BF),
        in_specs=vmem(1),
        out_specs=pl.BlockSpec(memory_space=pltpu.VMEM),
        compiler_params=params(),
        name="total",
    )(exchange(partial, "tensor"))
    shrunk = exchange(summed, "tensor")
    expanded = pl.pallas_call(
        expand_kernel,
        out_shape=jax.ShapeDtypeStruct((GROUPS, PAIR, WIDTH), BF),
        in_specs=vmem(3),
        out_specs=pl.BlockSpec(memory_space=pltpu.VMEM),
        scratch_shapes=[pltpu.VMEM((HELD * RANK, 256), BF)],
        compiler_params=params(),
        name="expand",
    )(shrunk, ids, b_pool.reshape(HELD * RANK, WIDTH).T)
    back = exchange(expanded, "replica").reshape(BUCKETS, WIDTH)
    base = jnp.dot(everything, weight, preferred_element_type=F32)
    return pl.pallas_call(
        final_kernel,
        out_shape=jax.ShapeDtypeStruct((ROWS, WIDTH), BF),
        in_specs=vmem(3),
        out_specs=pl.BlockSpec(memory_space=pltpu.VMEM),
        compiler_params=params(),
        name="final",
    )(dest.reshape(ROWS, 1), base, back)


def solution(mesh):
    in_specs = (
        P("replica", "tensor"),
        P(None, "tensor"),
        P("replica", None, "tensor"),
        P("replica", None, "tensor"),
        P("replica"),
        P(),
    )
    return jax.shard_map(
        body, mesh=mesh, in_specs=in_specs, out_specs=P("replica", "tensor"), check_vma=False
    )
```

```python
import jax
import jax.numpy as jnp
from jax import lax
from jax.experimental import pallas as pl
from jax.experimental.pallas import tpu as pltpu
from jax.sharding import Mesh, PartitionSpec as P

RANK = 64
SLOTS = 4
RPA = 16
PAIR = SLOTS * RPA
GROUPS = 32
HELD = 32
TENSOR = 16
ROWS = 768
WIDTH = 256
BUCKETS = GROUPS * PAIR
CHIPS = 16
PAY = 264
SCALE = 2.0

BF = jnp.bfloat16
F32 = jnp.float32
I32 = jnp.int32
NT = (((1,), (1,)), ((), ()))


def params():
    return pltpu.CompilerParams(vmem_limit_bytes=40 * 1024 * 1024)


def vmem(n):
    return [pl.BlockSpec(memory_space=pltpu.VMEM)] * n


def pack_kernel(dest_ref, local_ref, tokens_ref, out_ref):
    dest = dest_ref[...]
    local = local_ref[...]
    for b in range(8):
        at = lax.broadcasted_iota(I32, (256, ROWS), 0) + b * 256
        pick = (at == dest).astype(F32).astype(BF)
        rows = jnp.dot(pick, tokens_ref[...], preferred_element_type=F32).astype(BF)
        for j in range(2):
            for c in range(2):
                at = 128 * j + 64 * c
                out_ref[2 * b + j, 128 * c : 128 * c + 64, :] = rows[at : at + 64, 0:128]
                out_ref[2 * b + j, 128 * c + 64 : 128 * c + 128, :] = rows[at : at + 64, 128:256]
    group = lax.broadcasted_iota(I32, (GROUPS, ROWS), 0)
    to = (group == dest // PAIR).astype(F32).astype(BF)
    lane_slot = (lax.broadcasted_iota(I32, (128, ROWS), 0) % PAIR) // RPA
    slot = (dest % PAIR) // RPA
    first = dest % RPA == 0
    value = jnp.where((lane_slot == slot) & first, local.astype(F32), 0.0).astype(BF)
    ids = lax.dot_general(to, value, NT, preferred_element_type=F32)
    for z in range(CHIPS):
        two = [jnp.broadcast_to(ids[2 * z + c : 2 * z + c + 1, :], (4, 128)) for c in range(2)]
        out_ref[z, 256:264, :] = jnp.concatenate(two, axis=0).astype(BF)


def shrink_kernel(core_ref, pay_ref, own_ref, other_ref, out_ref, ids_ref):
    core = core_ref[0]
    low = lax.broadcasted_iota(I32, (8, 128), 1) < PAIR
    for pool_ref, c in ((own_ref, core), (other_ref, 1 - core)):
        at = pl.multiple_of(128 * c, 128)
        for b in range(4):
            parts = []
            marks = []
            for j in range(4):
                z = 4 * b + j
                parts.append(
                    jnp.concatenate(
                        [pay_ref[z, pl.ds(at, 64), :], pay_ref[z, pl.ds(at + 64, 64), :]], axis=1
                    )
                )
            for j in range(2):
                z = 4 * b + 2 * j
                both = jnp.where(
                    low, pay_ref[z, 256:264, :].astype(F32), pay_ref[z + 1, 256:264, :].astype(F32)
                )
                mark = jnp.where(c == 0, both[0:1, :], both[4:5, :]).astype(I32)
                ids_ref[8 * c + 2 * b + j] = jnp.broadcast_to(mark, (8, 128))
                marks.append(mark)
            rows = jnp.concatenate(parts, axis=0)
            mark = jnp.concatenate(marks, axis=1)
            total = jnp.zeros((RANK, 256), F32)
            for q in range(8):
                prod = lax.dot_general(
                    pool_ref[256 * q : 256 * q + 256, :], rows, NT, preferred_element_type=F32
                )
                for a in range(4):
                    total = total + jnp.where(mark == 4 * q + a, prod[64 * a : 64 * a + 64], 0.0)
            out_ref[8 * c + 2 * b] = total[:, 0:128].astype(BF)
            out_ref[8 * c + 2 * b + 1] = total[:, 128:256].astype(BF)


def sum_kernel(p_ref, out_ref):
    total = p_ref[0].astype(F32)
    for t in range(1, TENSOR):
        total = total + p_ref[t].astype(F32)
    mine = total.astype(BF)
    for t in range(TENSOR):
        out_ref[t] = mine


def expand_kernel(core_ref, s_ref, ids_ref, own_ref, other_ref, out_ref, m_ref):
    core = core_ref[0]
    for pool_ref, c in ((own_ref, core), (other_ref, 1 - core)):
        for b in range(4):
            at = 8 * c + 2 * b
            s = jnp.concatenate([s_ref[at], s_ref[at + 1]], axis=1).astype(F32)
            mark = jnp.concatenate([ids_ref[at][0:1], ids_ref[at + 1][0:1]], axis=1)
            for a in range(HELD):
                m_ref[64 * a : 64 * a + 64, :] = jnp.where(mark == a, s, 0.0).astype(BF)
            et = jnp.dot(pool_ref[...], m_ref[...], preferred_element_type=F32)
            rows = et.T.astype(BF)
            for j in range(4):
                out_ref[4 * b + j, c] = rows[64 * j : 64 * j + 64]


def final_kernel(dest_ref, base_ref, back_ref, out_ref):
    for b in range(3):
        at = lax.broadcasted_iota(I32, (256, BUCKETS), 1)
        pick = (at == dest_ref[256 * b : 256 * b + 256, :]).astype(F32).astype(BF)
        rows = jnp.dot(pick, back_ref[...], preferred_element_type=F32)
        out_ref[256 * b : 256 * b + 256, :] = (
            base_ref[256 * b : 256 * b + 256, :] + SCALE * rows
        ).astype(BF)


def route(row_adapter_index, adapter_pool_slot):
    table_ids = jnp.arange(adapter_pool_slot.shape[0], dtype=I32)
    pool_row = jnp.sum(
        jnp.where(row_adapter_index[:, None] == table_ids[None, :], adapter_pool_slot[None, :], 0),
        axis=1,
    )
    holder = pool_row // HELD
    order = jnp.arange(ROWS, dtype=I32)
    same = pool_row[:, None] == pool_row[None, :]
    place = jnp.sum(same & (order[None, :] < order[:, None]), axis=1)
    first = place == 0
    same_holder = holder[:, None] == holder[None, :]
    rank = jnp.sum(
        first[None, :] & same_holder & (pool_row[None, :] < pool_row[:, None]), axis=1
    )
    return (holder * SLOTS + rank) * RPA + place, pool_row % HELD


def exchange(x, axis):
    return lax.all_to_all(x, axis, split_axis=0, concat_axis=0, tiled=True)


def sibling(x):
    return lax.ppermute(x, "core", [(0, 1), (1, 0)])


def scalar():
    return pl.BlockSpec(memory_space=pltpu.SMEM)


def body(tokens, weight, a_pool, b_pool, row_adapter_index, adapter_pool_slot):
    everything = lax.all_gather(tokens, "tensor", axis=1, tiled=True)
    dest, local = route(row_adapter_index, adapter_pool_slot)
    payload = pl.pallas_call(
        pack_kernel,
        out_shape=jax.ShapeDtypeStruct((CHIPS, PAY, 128), BF),
        in_specs=vmem(3),
        out_specs=pl.BlockSpec(memory_space=pltpu.VMEM),
        compiler_params=params(),
        name="pack",
    )(dest.reshape(1, ROWS), local.reshape(1, ROWS), tokens)
    a_own = a_pool.reshape(HELD * RANK, WIDTH)
    b_own = b_pool.reshape(HELD * RANK, WIDTH).T
    a_other, b_other = sibling(a_own), sibling(b_own)
    core = lax.axis_index("core").astype(I32).reshape(1)
    arrived = exchange(payload, "z")
    partial, ids = pl.pallas_call(
        shrink_kernel,
        out_shape=(
            jax.ShapeDtypeStruct((TENSOR, RANK, 128), BF),
            jax.ShapeDtypeStruct((TENSOR, 8, 128), I32),
        ),
        in_specs=[scalar()] + vmem(3),
        out_specs=tuple(vmem(2)),
        compiler_params=params(),
        name="shrink",
    )(core, arrived, a_own, a_other)
    summed = pl.pallas_call(
        sum_kernel,
        out_shape=jax.ShapeDtypeStruct((TENSOR, RANK, 128), BF),
        in_specs=vmem(1),
        out_specs=pl.BlockSpec(memory_space=pltpu.VMEM),
        compiler_params=params(),
        name="total",
    )(exchange(partial, "tensor"))
    shrunk = exchange(summed, "tensor")
    expanded = pl.pallas_call(
        expand_kernel,
        out_shape=jax.ShapeDtypeStruct((CHIPS, 2, PAIR, WIDTH), BF),
        in_specs=[scalar()] + vmem(4),
        out_specs=pl.BlockSpec(memory_space=pltpu.VMEM),
        scratch_shapes=[pltpu.VMEM((HELD * RANK, 256), BF)],
        compiler_params=params(),
        name="expand",
    )(core, shrunk, ids, b_own, b_other)
    back = exchange(expanded, "z").reshape(BUCKETS, WIDTH)
    base = jnp.dot(everything, weight, preferred_element_type=F32)
    return pl.pallas_call(
        final_kernel,
        out_shape=jax.ShapeDtypeStruct((ROWS, WIDTH), BF),
        in_specs=vmem(3),
        out_specs=pl.BlockSpec(memory_space=pltpu.VMEM),
        compiler_params=params(),
        name="final",
    )(dest.reshape(ROWS, 1), base, back)


def solution(mesh):
    fine = Mesh(mesh.devices.reshape(CHIPS, 2, TENSOR), ("z", "core", "tensor"))
    group = ("z", "core")
    in_specs = (
        P(group, "tensor"),
        P(None, "tensor"),
        P(group, None, "tensor"),
        P(group, None, "tensor"),
        P(group),
        P(),
    )
    return jax.shard_map(
        body, mesh=fine, in_specs=in_specs, out_specs=P(group, "tensor"), check_vma=False
    )
```

```python
import jax
import jax.numpy as jnp
from jax import lax
from jax.experimental import pallas as pl
from jax.experimental.pallas import tpu as pltpu
from jax.sharding import Mesh, PartitionSpec as P

RANK = 64
SLOTS = 4
RPA = 16
PAIR = SLOTS * RPA
GROUPS = 32
HELD = 32
TENSOR = 16
ROWS = 768
WIDTH = 256
BUCKETS = GROUPS * PAIR
CHIPS = 16
PAY = 264
SCALE = 2.0

BF = jnp.bfloat16
F32 = jnp.float32
I32 = jnp.int32
NT = (((1,), (1,)), ((), ()))


def params():
    return pltpu.CompilerParams(vmem_limit_bytes=40 * 1024 * 1024)


def vmem(n):
    return [pl.BlockSpec(memory_space=pltpu.VMEM)] * n


def pack_kernel(dest_ref, local_ref, tokens_hbm, out_ref, tokens_ref, sem):
    bring = pltpu.make_async_copy(tokens_hbm, tokens_ref, sem.at[0])
    bring.start()
    dest = dest_ref[...]
    local = local_ref[...]
    line = lax.broadcasted_iota(I32, (8 * CHIPS, ROWS), 0)
    to = (line // 4 == dest // PAIR).astype(F32).astype(BF)
    lane_slot = (lax.broadcasted_iota(I32, (128, ROWS), 0) % PAIR) // RPA
    slot = (dest % PAIR) // RPA
    first = dest % RPA == 0
    value = jnp.where((lane_slot == slot) & first, local.astype(F32), 0.0).astype(BF)
    ids = lax.dot_general(to, value, NT, preferred_element_type=F32)
    for z in range(CHIPS):
        out_ref[z, 256:264, :] = ids[8 * z : 8 * z + 8, :].astype(BF)
    bring.wait()
    for b in range(8):
        at = lax.broadcasted_iota(I32, (256, ROWS), 0) + b * 256
        pick = (at == dest).astype(F32).astype(BF)
        rows = jnp.dot(pick, tokens_ref[...], preferred_element_type=F32).astype(BF)
        for j in range(2):
            for c in range(2):
                at = 128 * j + 64 * c
                out_ref[2 * b + j, 128 * c : 128 * c + 64, :] = rows[at : at + 64, 0:128]
                out_ref[2 * b + j, 128 * c + 64 : 128 * c + 128, :] = rows[at : at + 64, 128:256]


def shrink_kernel(core_ref, pay_ref, own_hbm, other_hbm, out_ref, ids_ref, pools, sem):
    core = core_ref[0]
    brings = [
        pltpu.make_async_copy(pool, pools.at[i], sem.at[i])
        for i, pool in enumerate((own_hbm, other_hbm))
    ]
    for bring in brings:
        bring.start()
    low = lax.broadcasted_iota(I32, (8, 128), 1) < PAIR
    for i, c in enumerate((core, 1 - core)):
        brings[i].wait()
        at = pl.multiple_of(128 * c, 128)
        for b in range(4):
            parts = []
            marks = []
            for j in range(4):
                z = 4 * b + j
                both = pay_ref[z, pl.ds(at, 128), :]
                parts.append(jnp.concatenate([both[0:64], both[64:128]], axis=1))
            for j in range(2):
                z = 4 * b + 2 * j
                both = jnp.where(
                    low, pay_ref[z, 256:264, :].astype(F32), pay_ref[z + 1, 256:264, :].astype(F32)
                )
                mark = jnp.where(c == 0, both[0:1, :], both[4:5, :])
                ids_ref[8 * c + 2 * b + j] = jnp.broadcast_to(mark, (8, 128))
                marks.append(mark)
            rows = jnp.concatenate(parts, axis=0)
            mark = jnp.broadcast_to(jnp.concatenate(marks, axis=1), (RANK, 256))
            total = jnp.zeros((RANK, 256), F32)
            for q in range(8):
                prod = lax.dot_general(
                    pools[i, 256 * q : 256 * q + 256, :], rows, NT, preferred_element_type=F32
                )
                for a in range(4):
                    total = jnp.where(mark == 4 * q + a, prod[64 * a : 64 * a + 64], total)
            out_ref[8 * c + 2 * b] = total[:, 0:128].astype(BF)
            out_ref[8 * c + 2 * b + 1] = total[:, 128:256].astype(BF)


def sum_kernel(p_ref, out_ref):
    total = p_ref[0].astype(F32)
    for t in range(1, TENSOR):
        total = total + p_ref[t].astype(F32)
    mine = total.astype(BF)
    for t in range(TENSOR):
        out_ref[t] = mine


def expand_kernel(core_ref, s_ref, ids_ref, own_hbm, other_hbm, out_ref, m_ref, pools, sem):
    core = core_ref[0]
    brings = [
        pltpu.make_async_copy(pool, pools.at[i], sem.at[i])
        for i, pool in enumerate((own_hbm, other_hbm))
    ]
    for bring in brings:
        bring.start()
    for i, c in enumerate((core, 1 - core)):
        for b in range(4):
            at = 8 * c + 2 * b
            s = jnp.concatenate([s_ref[at], s_ref[at + 1]], axis=1)
            mark = jnp.concatenate([ids_ref[at][0:1], ids_ref[at + 1][0:1]], axis=1)
            mark = jnp.broadcast_to(mark, (RANK, 256)).astype(BF)
            for a in range(HELD):
                m_ref[b % 2, 64 * a : 64 * a + 64, :] = jnp.where(
                    mark == jnp.asarray(a, BF), s, jnp.zeros_like(s)
                )
            if b == 0:
                brings[i].wait()
            et = jnp.dot(pools[i], m_ref[b % 2], preferred_element_type=F32)
            rows = et.T.astype(BF)
            for j in range(4):
                out_ref[4 * b + j, c] = rows[64 * j : 64 * j + 64]


def base_kernel(place_ref, *refs):
    xs, ws, outs = refs[0:4], refs[4:8], refs[8:12]
    place = place_ref[0]
    for s in range(4):
        for half in range(2):
            at = 384 * half
            total = jnp.zeros((384, WIDTH), F32)
            for d in range(4):
                row = pl.multiple_of(((place + d) % 4) * WIDTH, WIDTH)
                total = total + jnp.dot(
                    xs[d][at : at + 384, :],
                    ws[s][pl.ds(row, WIDTH), :],
                    preferred_element_type=F32,
                )
            outs[s][at : at + 384, :] = total.astype(outs[s].dtype)


def final_kernel(dest_ref, p0_hbm, p1_hbm, p2_hbm, p3_hbm, back_ref, out_ref, p0, pn, sem):
    brings = [pltpu.make_async_copy(p0_hbm, p0, sem.at[3])]
    for i, part in enumerate((p1_hbm, p2_hbm, p3_hbm)):
        brings.append(pltpu.make_async_copy(part, pn.at[i], sem.at[i]))
    for bring in brings:
        bring.start()
    for b in range(3):
        lo = 256 * b
        at = lax.broadcasted_iota(I32, (256, BUCKETS), 1)
        pick = (at == dest_ref[lo : lo + 256, :]).astype(F32).astype(BF)
        rows = jnp.dot(pick, back_ref[...], preferred_element_type=F32)
        if b == 0:
            for bring in brings:
                bring.wait()
        base = p0[lo : lo + 256, :]
        for i in range(3):
            base = base + pn[i, lo : lo + 256, :].astype(F32)
        out_ref[lo : lo + 256, :] = (base + SCALE * rows).astype(BF)


def route(row_adapter_index, adapter_pool_slot):
    table_ids = jnp.arange(adapter_pool_slot.shape[0], dtype=I32)
    pool_row = jnp.sum(
        jnp.where(row_adapter_index[:, None] == table_ids[None, :], adapter_pool_slot[None, :], 0),
        axis=1,
    )
    holder = pool_row // HELD
    order = jnp.arange(ROWS, dtype=I32)
    same = pool_row[:, None] == pool_row[None, :]
    place = jnp.sum(same & (order[None, :] < order[:, None]), axis=1)
    first = place == 0
    same_holder = holder[:, None] == holder[None, :]
    rank = jnp.sum(
        first[None, :] & same_holder & (pool_row[None, :] < pool_row[:, None]), axis=1
    )
    return (holder * SLOTS + rank) * RPA + place, pool_row % HELD


def exchange(x, axis):
    return lax.all_to_all(x, axis, split_axis=0, concat_axis=0, tiled=True)


def sibling(x):
    return lax.ppermute(x, "core", [(0, 1), (1, 0)])


def scalar():
    return pl.BlockSpec(memory_space=pltpu.SMEM)


def hbm(n):
    return [pl.BlockSpec(memory_space=pltpu.HBM)] * n


def turn(x, axis, step):
    return lax.ppermute(x, axis, [(i, (i + step) % 4) for i in range(4)])


def body(tokens, weight, a_pool, b_pool, row_adapter_index, adapter_pool_slot):
    tensor = ("y", "x")
    y = lax.axis_index("y")
    core = lax.axis_index("core").astype(I32).reshape(1)
    dest, local = route(row_adapter_index, adapter_pool_slot)
    payload = pl.pallas_call(
        pack_kernel,
        out_shape=jax.ShapeDtypeStruct((CHIPS, PAY, 128), BF),
        in_specs=vmem(2) + hbm(1),
        out_specs=pl.BlockSpec(memory_space=pltpu.VMEM),
        scratch_shapes=[pltpu.VMEM((ROWS, WIDTH), BF), pltpu.SemaphoreType.DMA((1,))],
        compiler_params=params(),
        name="pack",
    )(dest.reshape(1, ROWS), local.reshape(1, ROWS), tokens)
    tokens, weight, a_pool, b_pool, payload = lax.optimization_barrier(
        (tokens, weight, a_pool, b_pool, payload)
    )
    a_own = a_pool.reshape(HELD * RANK, WIDTH)
    b_own = b_pool.reshape(HELD * RANK, WIDTH).T
    a_other, b_other = sibling(a_own), sibling(b_own)
    arrived = exchange(payload, "z")
    xs = [tokens] + [turn(tokens, "x", -d) for d in range(1, 4)]
    ws = []
    for s in range(4):
        mine = lax.dynamic_slice(weight, (((y - s) % 4) * 4 * WIDTH, 0), (4 * WIDTH, WIDTH))
        ws.append(turn(mine, "y", -s) if s else mine)
    parts = pl.pallas_call(
        base_kernel,
        out_shape=tuple(jax.ShapeDtypeStruct((ROWS, WIDTH), BF if s else F32) for s in range(4)),
        in_specs=[scalar()] + vmem(8),
        out_specs=tuple(vmem(4)),
        compiler_params=params(),
        cost_estimate=pl.CostEstimate(
            flops=2 * ROWS * 16 * WIDTH * WIDTH, bytes_accessed=6 * 2**20, transcendentals=0
        ),
        name="base",
    )(lax.axis_index("x").astype(I32).reshape(1), *xs, *ws)
    arrived, *parts = lax.optimization_barrier((arrived, *parts))
    partial, ids = pl.pallas_call(
        shrink_kernel,
        out_shape=(
            jax.ShapeDtypeStruct((TENSOR, RANK, 128), BF),
            jax.ShapeDtypeStruct((TENSOR, 8, 128), F32),
        ),
        in_specs=[scalar()] + vmem(1) + hbm(2),
        out_specs=tuple(vmem(2)),
        scratch_shapes=[pltpu.VMEM((2, HELD * RANK, WIDTH), BF), pltpu.SemaphoreType.DMA((2,))],
        compiler_params=params(),
        name="shrink",
    )(core, arrived, a_own, a_other)
    summed = pl.pallas_call(
        sum_kernel,
        out_shape=jax.ShapeDtypeStruct((TENSOR, RANK, 128), BF),
        in_specs=vmem(1),
        out_specs=pl.BlockSpec(memory_space=pltpu.VMEM),
        compiler_params=params(),
        name="total",
    )(exchange(partial, tensor))
    shrunk = exchange(summed, tensor)
    expanded = pl.pallas_call(
        expand_kernel,
        out_shape=jax.ShapeDtypeStruct((CHIPS, 2, PAIR, WIDTH), BF),
        in_specs=[scalar()] + vmem(2) + hbm(2),
        out_specs=pl.BlockSpec(memory_space=pltpu.VMEM),
        scratch_shapes=[
            pltpu.VMEM((2, HELD * RANK, 256), BF),
            pltpu.VMEM((2, WIDTH, HELD * RANK), BF),
            pltpu.SemaphoreType.DMA((2,)),
        ],
        compiler_params=params(),
        name="expand",
    )(core, shrunk, ids, b_own, b_other)
    p0, p1, p2, p3, expanded = lax.optimization_barrier((*parts, expanded))
    back = exchange(expanded, "z").reshape(BUCKETS, WIDTH)
    sums = [turn(p, "y", s) for s, p in ((1, p1), (2, p2), (3, p3))]
    return pl.pallas_call(
        final_kernel,
        out_shape=jax.ShapeDtypeStruct((ROWS, WIDTH), BF),
        in_specs=vmem(1) + hbm(4) + vmem(1),
        out_specs=pl.BlockSpec(memory_space=pltpu.VMEM),
        scratch_shapes=[
            pltpu.VMEM((ROWS, WIDTH), F32),
            pltpu.VMEM((3, ROWS, WIDTH), BF),
            pltpu.SemaphoreType.DMA((4,)),
        ],
        compiler_params=params(),
        name="final",
    )(dest.reshape(ROWS, 1), p0, *sums, back)


def solution(mesh):
    fine = Mesh(mesh.devices.reshape(CHIPS, 2, 4, 4), ("z", "core", "y", "x"))
    group = ("z", "core")
    tensor = ("y", "x")
    in_specs = (
        P(group, tensor),
        P(None, tensor),
        P(group, None, tensor),
        P(group, None, tensor),
        P(group),
        P(),
    )
    return jax.shard_map(
        body, mesh=fine, in_specs=in_specs, out_specs=P(group, tensor), check_vma=False
    )
```

```python
import jax
import jax.numpy as jnp
from jax import lax
from jax.experimental import pallas as pl
from jax.experimental.pallas import tpu as pltpu
from jax.sharding import Mesh, PartitionSpec as P

RANK = 64
SLOTS = 4
RPA = 16
PAIR = SLOTS * RPA
GROUPS = 32
HELD = 32
TENSOR = 16
ROWS = 768
WIDTH = 256
BUCKETS = GROUPS * PAIR
CHIPS = 16
PAY = 264
SCALE = 2.0

BF = jnp.bfloat16
F32 = jnp.float32
I32 = jnp.int32
NT = (((1,), (1,)), ((), ()))


def params():
    return pltpu.CompilerParams(vmem_limit_bytes=40 * 1024 * 1024)


def vmem(n):
    return [pl.BlockSpec(memory_space=pltpu.VMEM)] * n


def across(row):
    return jnp.broadcast_to(row, (128, ROWS)).T[:, 0:1]


def pack_kernel(index_ref, slot_ref, tokens_hbm, pay_hbm, dest_ref, tokens_ref, pay_ref, sem, out_sem):
    bring = pltpu.make_async_copy(tokens_hbm, tokens_ref, sem.at[0])
    bring.start()
    adapters = slot_ref.shape[1]
    table = slot_ref[...]
    line = lax.broadcasted_iota(I32, (8, adapters), 0)
    table = jnp.where(line == 0, table >> 5, table & 31).astype(F32).astype(BF)
    named = lax.broadcasted_iota(I32, (adapters, ROWS), 0) == index_ref[...]
    found = jnp.dot(table, named.astype(F32).astype(BF), preferred_element_type=F32)
    holder, local = found[0:1], found[1:2]
    pool_row = holder * HELD + local
    pool_col = across(pool_row)
    shape = (ROWS, ROWS)
    before = lax.broadcasted_iota(I32, shape, 0) < lax.broadcasted_iota(I32, shape, 1)
    same = (pool_col == pool_row) & before
    place = jnp.sum(same.astype(F32), axis=0, keepdims=True)
    first_col = jnp.where(across(place) == 0, pool_col, -1.0)
    lower = (first_col >= holder * HELD) & (first_col < pool_row)
    rank = jnp.sum(lower.astype(F32), axis=0, keepdims=True)
    dest = ((holder * SLOTS + rank) * RPA + place).astype(I32)
    dest_ref[...] = dest
    line = lax.broadcasted_iota(I32, (8 * CHIPS, ROWS), 0) >> 2
    to = (line == holder.astype(I32)).astype(F32).astype(BF)
    lane_slot = (lax.broadcasted_iota(I32, (128, ROWS), 0) & (PAIR - 1)) >> 4
    value = jnp.where((lane_slot == rank.astype(I32)) & (place == 0), local, 0.0).astype(BF)
    ids = lax.dot_general(to, value, NT, preferred_element_type=F32)
    for z in range(CHIPS):
        pay_ref[z, 256:264, :] = ids[8 * z : 8 * z + 8, :].astype(BF)
    bring.wait()
    sends = []
    for b in range(8):
        at = lax.broadcasted_iota(I32, (256, ROWS), 0) + b * 256
        pick = (at == dest).astype(F32).astype(BF)
        rows = jnp.dot(pick, tokens_ref[...], preferred_element_type=F32).astype(BF)
        for j in range(2):
            for c in range(2):
                at = 128 * j + 64 * c
                pay_ref[2 * b + j, 128 * c : 128 * c + 64, :] = rows[at : at + 64, 0:128]
                pay_ref[2 * b + j, 128 * c + 64 : 128 * c + 128, :] = rows[at : at + 64, 128:256]
        two = pl.ds(2 * b, 2)
        sends.append(pltpu.make_async_copy(pay_ref.at[two], pay_hbm.at[two], out_sem.at[b]))
        sends[-1].start()
    for send in sends:
        send.wait()


def shrink_kernel(core_ref, pay_ref, own_hbm, other_hbm, out_ref, ids_ref, pools, sem):
    core = core_ref[0]
    brings = [
        pltpu.make_async_copy(pool, pools.at[i], sem.at[i])
        for i, pool in enumerate((own_hbm, other_hbm))
    ]
    for bring in brings:
        bring.start()
    low = lax.broadcasted_iota(I32, (8, 128), 1) < PAIR
    for i, c in enumerate((core, 1 - core)):
        brings[i].wait()
        at = pl.multiple_of(128 * c, 128)
        for b in range(4):
            parts = []
            marks = []
            for j in range(4):
                z = 4 * b + j
                both = pay_ref[z, pl.ds(at, 128), :]
                parts.append(jnp.concatenate([both[0:64], both[64:128]], axis=1))
            for j in range(2):
                z = 4 * b + 2 * j
                both = jnp.where(
                    low, pay_ref[z, 256:264, :].astype(F32), pay_ref[z + 1, 256:264, :].astype(F32)
                )
                mark = jnp.where(c == 0, both[0:1, :], both[4:5, :])
                ids_ref[8 * c + 2 * b + j] = jnp.broadcast_to(mark, (8, 128))
                marks.append(mark)
            rows = jnp.concatenate(parts, axis=0)
            mark = jnp.broadcast_to(jnp.concatenate(marks, axis=1), (RANK, 256))
            total = jnp.zeros((RANK, 256), F32)
            for q in range(8):
                prod = lax.dot_general(
                    pools[i, 256 * q : 256 * q + 256, :], rows, NT, preferred_element_type=F32
                )
                for a in range(4):
                    total = jnp.where(mark == 4 * q + a, prod[64 * a : 64 * a + 64], total)
            out_ref[8 * c + 2 * b] = total[:, 0:128].astype(BF)
            out_ref[8 * c + 2 * b + 1] = total[:, 128:256].astype(BF)


def sum_kernel(p_ref, out_ref):
    total = p_ref[0].astype(F32)
    for t in range(1, TENSOR):
        total = total + p_ref[t].astype(F32)
    mine = total.astype(BF)
    for t in range(TENSOR):
        out_ref[t] = mine


def marks_kernel(ids_ref, pool_hbm, out_ref):
    high = (lax.broadcasted_iota(I32, (128, 128), 1) >= RANK).astype(F32)
    for t in range(TENSOR):
        column = jnp.broadcast_to(ids_ref[t][0:1], (128, 128)).T
        out_ref[t] = (column - high).astype(BF)


def expand_kernel(core_ref, s_ref, marks_ref, own_hbm, other_hbm, out_hbm, m_ref, pools, rows_ref, sem, out_sem):
    core = core_ref[0]
    brings = [
        pltpu.make_async_copy(pool, pools.at[i], sem.at[i])
        for i, pool in enumerate((own_hbm, other_hbm))
    ]
    for bring in brings:
        bring.start()
    sends = []
    for i, c in enumerate((core, 1 - core)):
        for h in range(2):
            for k in range(4):
                at = 8 * c + 4 * h + k
                s = s_ref[at].astype(F32)
                s = jnp.concatenate([s, s], axis=0).T.astype(BF)
                mark = marks_ref[at]
                for j in range(HELD // 2):
                    m_ref[h, 128 * k : 128 * k + 128, 128 * j : 128 * j + 128] = jnp.where(
                        mark == jnp.asarray(2 * j, BF), s, jnp.zeros_like(s)
                    )
            if h == 0:
                brings[i].wait()
            e = jnp.dot(m_ref[h], pools[i], preferred_element_type=F32)
            rows_ref[i, 8 * h : 8 * h + 8] = e.astype(BF).reshape(8, PAIR, WIDTH)
            part = pl.ds(8 * h, 8)
            sends.append(
                pltpu.make_async_copy(
                    rows_ref.at[i, part], out_hbm.at[part, c], out_sem.at[2 * i + h]
                )
            )
            sends[-1].start()
    for send in sends:
        send.wait()


def base_kernel(place_ref, *refs):
    xs, ws, outs = refs[0:4], refs[4:8], refs[8:12]
    place = place_ref[0]
    for s in range(4):
        for half in range(2):
            at = 384 * half
            total = jnp.zeros((384, WIDTH), F32)
            for d in range(4):
                row = pl.multiple_of(((place + d) % 4) * WIDTH, WIDTH)
                total = total + jnp.dot(
                    xs[d][at : at + 384, :],
                    ws[s][pl.ds(row, WIDTH), :],
                    preferred_element_type=F32,
                )
            outs[s][at : at + 384, :] = total.astype(outs[s].dtype)


def ready_kernel(p0_ref, p1_ref, p2_ref, p3_ref, base_ref):
    base = p0_ref[...]
    for part_ref in (p1_ref, p2_ref, p3_ref):
        base = base + part_ref[...].astype(F32)
    base_ref[...] = base


def final_kernel(dest_ref, base_ref, back_ref, out_ref):
    for b in range(3):
        lo = 256 * b
        at = lax.broadcasted_iota(I32, (256, BUCKETS), 1)
        pick = (at == dest_ref[lo : lo + 256, :]).astype(F32).astype(BF)
        rows = jnp.dot(pick, back_ref[...], preferred_element_type=F32)
        out_ref[lo : lo + 256, :] = (base_ref[lo : lo + 256, :] + SCALE * rows).astype(BF)


def exchange(x, axis):
    return lax.all_to_all(x, axis, split_axis=0, concat_axis=0, tiled=True)


def sibling(x):
    return lax.ppermute(x, "core", [(0, 1), (1, 0)])


def scalar():
    return pl.BlockSpec(memory_space=pltpu.SMEM)


def hbm(n):
    return [pl.BlockSpec(memory_space=pltpu.HBM)] * n


def turn(x, axis, step):
    return lax.ppermute(x, axis, [(i, (i + step) % 4) for i in range(4)])


def body(tokens, weight, a_pool, b_pool, row_adapter_index, adapter_pool_slot):
    tensor = ("y", "x")
    y = lax.axis_index("y")
    core = lax.axis_index("core").astype(I32).reshape(1)
    payload, dest = pl.pallas_call(
        pack_kernel,
        out_shape=(
            jax.ShapeDtypeStruct((CHIPS, PAY, 128), BF),
            jax.ShapeDtypeStruct((1, ROWS), I32),
        ),
        in_specs=vmem(2) + hbm(1),
        out_specs=tuple(hbm(1) + vmem(1)),
        scratch_shapes=[
            pltpu.VMEM((ROWS, WIDTH), BF),
            pltpu.VMEM((CHIPS, PAY, 128), BF),
            pltpu.SemaphoreType.DMA((1,)),
            pltpu.SemaphoreType.DMA((8,)),
        ],
        compiler_params=params(),
        name="pack",
    )(row_adapter_index.reshape(1, ROWS), adapter_pool_slot.reshape(1, -1), tokens)
    tokens, weight, a_pool, b_pool, payload = lax.optimization_barrier(
        (tokens, weight, a_pool, b_pool, payload)
    )
    a_own = a_pool.reshape(HELD * RANK, WIDTH)
    b_own = b_pool.reshape(HELD * RANK, WIDTH)
    a_other, b_other = sibling(a_own), sibling(b_own)
    arrived = exchange(payload, "z")
    xs = [tokens] + [turn(tokens, "x", -d) for d in range(1, 4)]
    ws = []
    for s in range(4):
        mine = lax.dynamic_slice(weight, (((y - s) % 4) * 4 * WIDTH, 0), (4 * WIDTH, WIDTH))
        ws.append(turn(mine, "y", -s) if s else mine)
    parts = pl.pallas_call(
        base_kernel,
        out_shape=tuple(jax.ShapeDtypeStruct((ROWS, WIDTH), BF if s else F32) for s in range(4)),
        in_specs=[scalar()] + vmem(8),
        out_specs=tuple(vmem(4)),
        compiler_params=params(),
        cost_estimate=pl.CostEstimate(
            flops=2 * ROWS * 16 * WIDTH * WIDTH, bytes_accessed=6 * 2**20, transcendentals=0
        ),
        name="base",
    )(lax.axis_index("x").astype(I32).reshape(1), *xs, *ws)
    partial, ids = pl.pallas_call(
        shrink_kernel,
        out_shape=(
            jax.ShapeDtypeStruct((TENSOR, RANK, 128), BF),
            jax.ShapeDtypeStruct((TENSOR, 8, 128), F32),
        ),
        in_specs=[scalar()] + vmem(1) + hbm(2),
        out_specs=tuple(vmem(2)),
        scratch_shapes=[pltpu.VMEM((2, HELD * RANK, WIDTH), BF), pltpu.SemaphoreType.DMA((2,))],
        compiler_params=params(),
        name="shrink",
    )(core, arrived, a_own, a_other)
    summed = pl.pallas_call(
        sum_kernel,
        out_shape=jax.ShapeDtypeStruct((TENSOR, RANK, 128), BF),
        in_specs=vmem(1),
        out_specs=pl.BlockSpec(memory_space=pltpu.VMEM),
        compiler_params=params(),
        name="total",
    )(exchange(partial, tensor))
    shrunk = exchange(summed, tensor)
    marks = pl.pallas_call(
        marks_kernel,
        out_shape=jax.ShapeDtypeStruct((TENSOR, 128, 128), BF),
        in_specs=vmem(1) + hbm(1),
        out_specs=pl.BlockSpec(memory_space=pltpu.VMEM),
        compiler_params=params(),
        name="marks",
    )(ids, b_own)
    expanded = pl.pallas_call(
        expand_kernel,
        out_shape=jax.ShapeDtypeStruct((CHIPS, 2, PAIR, WIDTH), BF),
        in_specs=[scalar()] + vmem(2) + hbm(2),
        out_specs=pl.BlockSpec(memory_space=pltpu.HBM),
        scratch_shapes=[
            pltpu.VMEM((2, 512, HELD * RANK), BF),
            pltpu.VMEM((2, HELD * RANK, WIDTH), BF),
            pltpu.VMEM((2, CHIPS, PAIR, WIDTH), BF),
            pltpu.SemaphoreType.DMA((2,)),
            pltpu.SemaphoreType.DMA((4,)),
        ],
        compiler_params=params(),
        name="expand",
    )(core, shrunk, marks, b_own, b_other)
    p0, p1, p2, p3, expanded = lax.optimization_barrier((*parts, expanded))
    back = exchange(expanded, "z").reshape(BUCKETS, WIDTH)
    sums = [turn(p, "y", s) for s, p in ((1, p1), (2, p2), (3, p3))]
    base = pl.pallas_call(
        ready_kernel,
        out_shape=jax.ShapeDtypeStruct((ROWS, WIDTH), F32),
        in_specs=vmem(4),
        out_specs=pl.BlockSpec(memory_space=pltpu.VMEM),
        compiler_params=params(),
        name="ready",
    )(p0, *sums)
    return pl.pallas_call(
        final_kernel,
        out_shape=jax.ShapeDtypeStruct((ROWS, WIDTH), BF),
        in_specs=vmem(3),
        out_specs=pl.BlockSpec(memory_space=pltpu.VMEM),
        compiler_params=params(),
        name="final",
    )(dest.reshape(ROWS, 1), base, back)


def solution(mesh):
    fine = Mesh(mesh.devices.reshape(CHIPS, 2, 4, 4), ("z", "core", "y", "x"))
    group = ("z", "core")
    tensor = ("y", "x")
    in_specs = (
        P(group, tensor),
        P(None, tensor),
        P(group, None, tensor),
        P(group, None, tensor),
        P(group),
        P(),
    )
    return jax.shard_map(
        body, mesh=fine, in_specs=in_specs, out_specs=P(group, tensor), check_vma=False
    )
```

```python
import jax
import jax.numpy as jnp
from jax import lax
from jax.experimental import pallas as pl
from jax.experimental.pallas import tpu as pltpu
from jax.sharding import Mesh, PartitionSpec as P

RANK = 64
SLOTS = 4
RPA = 16
PAIR = SLOTS * RPA
GROUPS = 32
HELD = 32
TENSOR = 16
ROWS = 768
WIDTH = 256
BUCKETS = GROUPS * PAIR
CHIPS = 16
PAY = 264
SCALE = 2.0

BF = jnp.bfloat16
F32 = jnp.float32
I32 = jnp.int32
NT = (((1,), (1,)), ((), ()))


def params():
    return pltpu.CompilerParams(vmem_limit_bytes=40 * 1024 * 1024)


def vmem(n):
    return [pl.BlockSpec(memory_space=pltpu.VMEM)] * n


def across(row):
    return jnp.broadcast_to(row, (128, ROWS)).T[:, 0:1]


def pack_kernel(table_ref, tokens_hbm, pay_hbm, dest_ref, tokens_ref, pay_ref, sem, out_sem):
    bring = pltpu.make_async_copy(tokens_hbm, tokens_ref, sem.at[0])
    bring.start()
    adapters = table_ref.shape[1] - ROWS
    index = table_ref[:, 0:ROWS]
    table = table_ref[:, ROWS:]
    line = lax.broadcasted_iota(I32, (8, adapters), 0)
    table = jnp.where(line == 0, table >> 5, table & 31).astype(F32).astype(BF)
    named = lax.broadcasted_iota(I32, (adapters, ROWS), 0) == index
    found = jnp.dot(table, named.astype(F32).astype(BF), preferred_element_type=F32)
    holder, local = found[0:1], found[1:2]
    pool_row = holder * HELD + local
    pool_col = across(pool_row)
    shape = (ROWS, ROWS)
    before = lax.broadcasted_iota(I32, shape, 0) < lax.broadcasted_iota(I32, shape, 1)
    same = (pool_col == pool_row) & before
    place = jnp.sum(same.astype(F32), axis=0, keepdims=True)
    first_col = jnp.where(across(place) == 0, pool_col, -1.0)
    lower = (first_col >= holder * HELD) & (first_col < pool_row)
    rank = jnp.sum(lower.astype(F32), axis=0, keepdims=True)
    dest = ((holder * SLOTS + rank) * RPA + place).astype(I32)
    dest_ref[...] = dest
    line = lax.broadcasted_iota(I32, (8 * CHIPS, ROWS), 0) >> 2
    to = (line == holder.astype(I32)).astype(F32).astype(BF)
    lane_slot = (lax.broadcasted_iota(I32, (128, ROWS), 0) & (PAIR - 1)) >> 4
    value = jnp.where((lane_slot == rank.astype(I32)) & (place == 0), local, 0.0).astype(BF)
    ids = lax.dot_general(to, value, NT, preferred_element_type=F32)
    for z in range(CHIPS):
        pay_ref[z, 256:264, :] = ids[8 * z : 8 * z + 8, :].astype(BF)
    bring.wait()
    sends = []
    for b in range(8):
        at = lax.broadcasted_iota(I32, (256, ROWS), 0) + b * 256
        pick = (at == dest).astype(F32).astype(BF)
        rows = jnp.dot(pick, tokens_ref[...], preferred_element_type=F32).astype(BF)
        for j in range(2):
            for c in range(2):
                at = 128 * j + 64 * c
                pay_ref[2 * b + j, 128 * c : 128 * c + 64, :] = rows[at : at + 64, 0:128]
                pay_ref[2 * b + j, 128 * c + 64 : 128 * c + 128, :] = rows[at : at + 64, 128:256]
        two = pl.ds(2 * b, 2)
        sends.append(pltpu.make_async_copy(pay_ref.at[two], pay_hbm.at[two], out_sem.at[b]))
        sends[-1].start()
    for send in sends:
        send.wait()


def shrink_kernel(core_ref, pay_ref, own_ref, other_hbm, out_ref, ids_ref, other_ref, sem):
    core = core_ref[0]
    bring = pltpu.make_async_copy(other_hbm, other_ref, sem.at[0])
    bring.start()
    low = lax.broadcasted_iota(I32, (8, 128), 1) < PAIR
    for pool_ref, c in ((own_ref, core), (other_ref, 1 - core)):
        if pool_ref is other_ref:
            bring.wait()
        at = pl.multiple_of(128 * c, 128)
        for b in range(4):
            parts = []
            marks = []
            for j in range(4):
                z = 4 * b + j
                both = pay_ref[z, pl.ds(at, 128), :]
                parts.append(jnp.concatenate([both[0:64], both[64:128]], axis=1))
            for j in range(2):
                z = 4 * b + 2 * j
                both = jnp.where(
                    low, pay_ref[z, 256:264, :].astype(F32), pay_ref[z + 1, 256:264, :].astype(F32)
                )
                mark = jnp.where(c == 0, both[0:1, :], both[4:5, :])
                ids_ref[8 * c + 2 * b + j] = jnp.broadcast_to(mark, (8, 128))
                marks.append(mark)
            rows = jnp.concatenate(parts, axis=0)
            mark = jnp.broadcast_to(jnp.concatenate(marks, axis=1), (RANK, 256))
            total = jnp.zeros((RANK, 256), F32)
            for q in range(8):
                prod = lax.dot_general(
                    pool_ref[256 * q : 256 * q + 256, :], rows, NT, preferred_element_type=F32
                )
                for a in range(4):
                    total = jnp.where(mark == 4 * q + a, prod[64 * a : 64 * a + 64], total)
            out_ref[8 * c + 2 * b] = total[:, 0:128].astype(BF)
            out_ref[8 * c + 2 * b + 1] = total[:, 128:256].astype(BF)


def sum_kernel(p_ref, out_ref):
    total = p_ref[0].astype(F32)
    for t in range(1, TENSOR):
        total = total + p_ref[t].astype(F32)
    mine = total.astype(BF)
    for t in range(TENSOR):
        out_ref[t] = mine


def marks_kernel(ids_ref, pool_hbm, out_ref):
    high = (lax.broadcasted_iota(I32, (128, 128), 1) >= RANK).astype(F32)
    for t in range(TENSOR):
        column = jnp.broadcast_to(ids_ref[t][0:1], (128, 128)).T
        out_ref[t] = (column - high).astype(BF)


def expand_kernel(
    core_ref, s_ref, marks_ref, own_ref, other_hbm, out_hbm, other_ref, rows_ref, sem, out_sem
):
    core = core_ref[0]
    bring = pltpu.make_async_copy(other_hbm, other_ref, sem.at[0])
    bring.start()
    sends = []
    for i, (pool_ref, c) in enumerate(((own_ref, core), (other_ref, 1 - core))):
        if i:
            bring.wait()
        for b in range(4):
            at = 8 * c + 2 * b
            s, mark = [], []
            for k in range(2):
                one = s_ref[at + k].astype(F32)
                s.append(jnp.concatenate([one, one], axis=0).T.astype(BF))
                mark.append(marks_ref[at + k])
            s, mark = jnp.concatenate(s, axis=0), jnp.concatenate(mark, axis=0)
            m = jnp.concatenate(
                [
                    jnp.where(mark == jnp.asarray(2 * j, BF), s, jnp.zeros_like(s))
                    for j in range(HELD // 2)
                ],
                axis=1,
            )
            e = jnp.dot(m, pool_ref[...], preferred_element_type=F32)
            part = pl.ds(4 * b, 4)
            rows_ref[i, part] = e.astype(BF).reshape(4, PAIR, WIDTH)
            sends.append(
                pltpu.make_async_copy(
                    rows_ref.at[i, part], out_hbm.at[part, c], out_sem.at[4 * i + b]
                )
            )
            sends[-1].start()
    for send in sends:
        send.wait()


def base_kernel(place_ref, *refs):
    outs, (xs, ws, sem) = refs[8:12], refs[12:15]
    brings = [
        pltpu.make_async_copy(refs[i], xs.at[i] if i < 4 else ws.at[i - 4], sem.at[i])
        for i in range(8)
    ]
    for i in (0, 1, 2, 3, 4, 5, 6, 7):
        brings[i].start()
    for bring in brings[0:4]:
        bring.wait()
    place = place_ref[0]
    for s in range(4):
        brings[4 + s].wait()
        for half in range(2):
            at = 384 * half
            total = jnp.zeros((384, WIDTH), F32)
            for d in range(4):
                row = pl.multiple_of(((place + d) & 3) * WIDTH, WIDTH)
                total = total + jnp.dot(
                    xs[d, at : at + 384, :],
                    ws[s, pl.ds(row, WIDTH), :],
                    preferred_element_type=F32,
                )
            outs[s][at : at + 384, :] = total.astype(outs[s].dtype)


def ready_kernel(p0_ref, p1_ref, p2_ref, p3_ref, base_ref):
    base = p0_ref[...]
    for part_ref in (p1_ref, p2_ref, p3_ref):
        base = base + part_ref[...].astype(F32)
    base_ref[...] = base


def final_kernel(dest_ref, base_ref, back_ref, out_ref):
    for b in range(3):
        lo = 256 * b
        at = lax.broadcasted_iota(I32, (256, BUCKETS), 1)
        pick = (at == dest_ref[lo : lo + 256, :]).astype(F32).astype(BF)
        rows = jnp.dot(pick, back_ref[...], preferred_element_type=F32)
        out_ref[lo : lo + 256, :] = (base_ref[lo : lo + 256, :] + SCALE * rows).astype(BF)


def exchange(x, axis):
    return lax.all_to_all(x, axis, split_axis=0, concat_axis=0, tiled=True)


def sibling(x):
    return lax.ppermute(x, "core", [(0, 1), (1, 0)])


def scalar():
    return pl.BlockSpec(memory_space=pltpu.SMEM)


def hbm(n):
    return [pl.BlockSpec(memory_space=pltpu.HBM)] * n


def turn(x, axis, step):
    return lax.ppermute(x, axis, [(i, (i + step) % 4) for i in range(4)])


def body(tokens, weight, a_pool, b_pool, row_adapter_index, adapter_pool_slot):
    tensor = ("y", "x")
    y = lax.axis_index("y")
    core = lax.axis_index("core").astype(I32).reshape(1)
    payload, dest = pl.pallas_call(
        pack_kernel,
        out_shape=(
            jax.ShapeDtypeStruct((CHIPS, PAY, 128), BF),
            jax.ShapeDtypeStruct((1, ROWS), I32),
        ),
        in_specs=vmem(1) + hbm(1),
        out_specs=tuple(hbm(1) + vmem(1)),
        scratch_shapes=[
            pltpu.VMEM((ROWS, WIDTH), BF),
            pltpu.VMEM((CHIPS, PAY, 128), BF),
            pltpu.SemaphoreType.DMA((1,)),
            pltpu.SemaphoreType.DMA((8,)),
        ],
        compiler_params=params(),
        name="pack",
    )(jnp.concatenate([row_adapter_index, adapter_pool_slot]).reshape(1, -1), tokens)
    tokens, weight, a_pool, b_pool, payload = lax.optimization_barrier(
        (tokens, weight, a_pool, b_pool, payload)
    )
    a_own = a_pool.reshape(HELD * RANK, WIDTH)
    b_own = b_pool.reshape(HELD * RANK, WIDTH)
    a_other, b_other = sibling(a_own), sibling(b_own)
    arrived = exchange(payload, "z")
    xs = [tokens] + [turn(tokens, "x", -d) for d in range(1, 4)]
    ws = []
    for s in range(4):
        mine = lax.dynamic_slice(weight, (((y - s) % 4) * 4 * WIDTH, 0), (4 * WIDTH, WIDTH))
        ws.append(turn(mine, "y", -s) if s else mine)
    parts = pl.pallas_call(
        base_kernel,
        out_shape=tuple(jax.ShapeDtypeStruct((ROWS, WIDTH), BF if s else F32) for s in range(4)),
        in_specs=[scalar()] + hbm(8),
        out_specs=tuple(vmem(4)),
        scratch_shapes=[
            pltpu.VMEM((4, ROWS, WIDTH), BF),
            pltpu.VMEM((4, 4 * WIDTH, WIDTH), BF),
            pltpu.SemaphoreType.DMA((8,)),
        ],
        compiler_params=params(),
        cost_estimate=pl.CostEstimate(
            flops=2 * ROWS * 16 * WIDTH * WIDTH, bytes_accessed=6 * 2**20, transcendentals=0
        ),
        name="base",
    )(lax.axis_index("x").astype(I32).reshape(1), *xs, *ws)
    partial, ids = pl.pallas_call(
        shrink_kernel,
        out_shape=(
            jax.ShapeDtypeStruct((TENSOR, RANK, 128), BF),
            jax.ShapeDtypeStruct((TENSOR, 8, 128), F32),
        ),
        in_specs=[scalar()] + vmem(2) + hbm(1),
        out_specs=tuple(vmem(2)),
        scratch_shapes=[pltpu.VMEM((HELD * RANK, WIDTH), BF), pltpu.SemaphoreType.DMA((1,))],
        compiler_params=params(),
        name="shrink",
    )(core, arrived, a_own, a_other)
    summed = pl.pallas_call(
        sum_kernel,
        out_shape=jax.ShapeDtypeStruct((TENSOR, RANK, 128), BF),
        in_specs=vmem(1),
        out_specs=pl.BlockSpec(memory_space=pltpu.VMEM),
        compiler_params=params(),
        name="total",
    )(exchange(partial, tensor))
    shrunk = exchange(summed, tensor)
    marks = pl.pallas_call(
        marks_kernel,
        out_shape=jax.ShapeDtypeStruct((TENSOR, 128, 128), BF),
        in_specs=vmem(1) + hbm(1),
        out_specs=pl.BlockSpec(memory_space=pltpu.VMEM),
        compiler_params=params(),
        name="marks",
    )(ids, b_own)
    expanded = pl.pallas_call(
        expand_kernel,
        out_shape=jax.ShapeDtypeStruct((CHIPS, 2, PAIR, WIDTH), BF),
        in_specs=[scalar()] + vmem(3) + hbm(1),
        out_specs=pl.BlockSpec(memory_space=pltpu.HBM),
        scratch_shapes=[
            pltpu.VMEM((HELD * RANK, WIDTH), BF),
            pltpu.VMEM((2, CHIPS, PAIR, WIDTH), BF),
            pltpu.SemaphoreType.DMA((1,)),
            pltpu.SemaphoreType.DMA((8,)),
        ],
        compiler_params=params(),
        name="expand",
    )(core, shrunk, marks, b_own, b_other)
    p0, p1, p2, p3, expanded = lax.optimization_barrier((*parts, expanded))
    back = exchange(expanded, "z").reshape(BUCKETS, WIDTH)
    sums = [turn(p, "y", s) for s, p in ((1, p1), (2, p2), (3, p3))]
    base = pl.pallas_call(
        ready_kernel,
        out_shape=jax.ShapeDtypeStruct((ROWS, WIDTH), F32),
        in_specs=vmem(4),
        out_specs=pl.BlockSpec(memory_space=pltpu.VMEM),
        compiler_params=params(),
        name="ready",
    )(p0, *sums)
    return pl.pallas_call(
        final_kernel,
        out_shape=jax.ShapeDtypeStruct((ROWS, WIDTH), BF),
        in_specs=vmem(3),
        out_specs=pl.BlockSpec(memory_space=pltpu.VMEM),
        compiler_params=params(),
        name="final",
    )(dest.reshape(ROWS, 1), base, back)


def solution(mesh):
    fine = Mesh(mesh.devices.reshape(CHIPS, 2, 4, 4), ("z", "core", "y", "x"))
    group = ("z", "core")
    tensor = ("y", "x")
    in_specs = (
        P(group, tensor),
        P(None, tensor),
        P(group, None, tensor),
        P(group, None, tensor),
        P(group),
        P(),
    )
    return jax.shard_map(
        body, mesh=fine, in_specs=in_specs, out_specs=P(group, tensor), check_vma=False
    )
```

```python
import jax
import jax.numpy as jnp
from jax import lax
from jax.experimental import pallas as pl
from jax.experimental.pallas import tpu as pltpu
from jax.sharding import Mesh, PartitionSpec as P

RANK = 64
SLOTS = 4
RPA = 16
PAIR = SLOTS * RPA
GROUPS = 32
HELD = 32
TENSOR = 16
ROWS = 768
WIDTH = 256
BUCKETS = GROUPS * PAIR
CHIPS = 16
PAY = 264
SCALE = 2.0

BF = jnp.bfloat16
F32 = jnp.float32
I32 = jnp.int32
NT = (((1,), (1,)), ((), ()))


def params():
    return pltpu.CompilerParams(vmem_limit_bytes=40 * 1024 * 1024)


def vmem(n):
    return [pl.BlockSpec(memory_space=pltpu.VMEM)] * n


def across(row):
    return jnp.broadcast_to(row, (128, ROWS)).T[:, 0:1]


def pack_kernel(table_ref, tokens_hbm, pay_hbm, dest_ref, tokens_ref, pay_ref, sem, out_sem):
    bring = pltpu.make_async_copy(tokens_hbm, tokens_ref, sem.at[0])
    bring.start()
    adapters = table_ref.shape[1] - ROWS
    index = table_ref[:, 0:ROWS]
    table = table_ref[:, ROWS:]
    line = lax.broadcasted_iota(I32, (8, adapters), 0)
    table = jnp.where(line == 0, table >> 5, table & 31).astype(F32).astype(BF)
    named = lax.broadcasted_iota(I32, (adapters, ROWS), 0) == index
    found = jnp.dot(table, named.astype(F32).astype(BF), preferred_element_type=F32)
    holder, local = found[0:1], found[1:2]
    pool_row = holder * HELD + local
    pool_col = across(pool_row)
    shape = (ROWS, ROWS)
    before = lax.broadcasted_iota(I32, shape, 0) < lax.broadcasted_iota(I32, shape, 1)
    same = (pool_col == pool_row) & before
    place = jnp.sum(same.astype(F32), axis=0, keepdims=True)
    first_col = jnp.where(across(place) == 0, pool_col, -1.0)
    lower = (first_col >= holder * HELD) & (first_col < pool_row)
    rank = jnp.sum(lower.astype(F32), axis=0, keepdims=True)
    dest = ((holder * SLOTS + rank) * RPA + place).astype(I32)
    dest_ref[...] = dest
    line = lax.broadcasted_iota(I32, (8 * CHIPS, ROWS), 0) >> 2
    to = (line == holder.astype(I32)).astype(F32).astype(BF)
    lane_slot = (lax.broadcasted_iota(I32, (128, ROWS), 0) & (PAIR - 1)) >> 4
    value = jnp.where((lane_slot == rank.astype(I32)) & (place == 0), local, 0.0).astype(BF)
    ids = lax.dot_general(to, value, NT, preferred_element_type=F32)
    for z in range(CHIPS):
        pay_ref[z, 256:264, :] = ids[8 * z : 8 * z + 8, :].astype(BF)
    bring.wait()
    sends = []
    for b in range(8):
        at = lax.broadcasted_iota(I32, (256, ROWS), 0) + b * 256
        pick = (at == dest).astype(F32).astype(BF)
        rows = jnp.dot(pick, tokens_ref[...], preferred_element_type=F32).astype(BF)
        for j in range(2):
            for c in range(2):
                at = 128 * j + 64 * c
                pay_ref[2 * b + j, 128 * c : 128 * c + 64, :] = rows[at : at + 64, 0:128]
                pay_ref[2 * b + j, 128 * c + 64 : 128 * c + 128, :] = rows[at : at + 64, 128:256]
        two = pl.ds(2 * b, 2)
        sends.append(pltpu.make_async_copy(pay_ref.at[two], pay_hbm.at[two], out_sem.at[b]))
        sends[-1].start()
    for send in sends:
        send.wait()


def shrink_kernel(core_ref, pay_ref, own_hbm, other_hbm, out_ref, ids_ref, pools, sem):
    core = core_ref[0]
    brings = [
        pltpu.make_async_copy(pool, pools.at[i], sem.at[i])
        for i, pool in enumerate((own_hbm, other_hbm))
    ]
    for bring in brings:
        bring.start()
    low = lax.broadcasted_iota(I32, (8, 128), 1) < PAIR
    for i, c in enumerate((core, 1 - core)):
        brings[i].wait()
        at = pl.multiple_of(128 * c, 128)
        for b in range(4):
            parts = []
            marks = []
            for j in range(4):
                z = 4 * b + j
                both = pay_ref[z, pl.ds(at, 128), :]
                parts.append(jnp.concatenate([both[0:64], both[64:128]], axis=1))
            for j in range(2):
                z = 4 * b + 2 * j
                both = jnp.where(
                    low, pay_ref[z, 256:264, :].astype(F32), pay_ref[z + 1, 256:264, :].astype(F32)
                )
                mark = jnp.where(c == 0, both[0:1, :], both[4:5, :])
                ids_ref[8 * c + 2 * b + j] = jnp.broadcast_to(mark, (8, 128))
                marks.append(mark)
            rows = jnp.concatenate(parts, axis=0)
            mark = jnp.broadcast_to(jnp.concatenate(marks, axis=1), (RANK, 256))
            total = jnp.zeros((RANK, 256), F32)
            for q in range(8):
                prod = lax.dot_general(
                    pools[i, 256 * q : 256 * q + 256, :], rows, NT, preferred_element_type=F32
                )
                for a in range(4):
                    total = jnp.where(mark == 4 * q + a, prod[64 * a : 64 * a + 64], total)
            out_ref[8 * c + 2 * b] = total[:, 0:128].astype(BF)
            out_ref[8 * c + 2 * b + 1] = total[:, 128:256].astype(BF)


def sum_kernel(p_ref, out_ref):
    total = p_ref[0].astype(F32)
    for t in range(1, TENSOR):
        total = total + p_ref[t].astype(F32)
    mine = total.astype(BF)
    for t in range(TENSOR):
        out_ref[t] = mine


def marks_kernel(ids_ref, pool_hbm, out_ref):
    high = (lax.broadcasted_iota(I32, (128, 128), 1) >= RANK).astype(F32)
    for t in range(TENSOR):
        column = jnp.broadcast_to(ids_ref[t][0:1], (128, 128)).T
        out_ref[t] = (column - high).astype(BF)


def expand_kernel(
    core_ref, s_ref, marks_ref, own_ref, other_hbm, out_hbm, other_ref, rows_ref, sem, out_sem
):
    core = core_ref[0]
    bring = pltpu.make_async_copy(other_hbm, other_ref, sem.at[0])
    bring.start()
    sends = []
    for i, (pool_ref, c) in enumerate(((own_ref, core), (other_ref, 1 - core))):
        if i:
            bring.wait()
        for b in range(4):
            at = 8 * c + 2 * b
            s, mark = [], []
            for k in range(2):
                one = s_ref[at + k].astype(F32)
                s.append(jnp.concatenate([one, one], axis=0).T.astype(BF))
                mark.append(marks_ref[at + k])
            s, mark = jnp.concatenate(s, axis=0), jnp.concatenate(mark, axis=0)
            m = jnp.concatenate(
                [
                    jnp.where(mark == jnp.asarray(2 * j, BF), s, jnp.zeros_like(s))
                    for j in range(HELD // 2)
                ],
                axis=1,
            )
            e = jnp.dot(m, pool_ref[...], preferred_element_type=F32)
            part = pl.ds(4 * b, 4)
            rows_ref[i, part] = e.astype(BF).reshape(4, PAIR, WIDTH)
            sends.append(
                pltpu.make_async_copy(
                    rows_ref.at[i, part], out_hbm.at[part, c], out_sem.at[4 * i + b]
                )
            )
            sends[-1].start()
    for send in sends:
        send.wait()


def base_kernel(place_ref, *refs):
    outs, (xs, ws, sem) = refs[6:8], refs[8:11]
    brings = [
        pltpu.make_async_copy(refs[i], xs.at[i] if i < 4 else ws.at[i - 4], sem.at[i])
        for i in range(6)
    ]
    for bring in brings:
        bring.start()
    for bring in brings[0:4]:
        bring.wait()
    place = place_ref[0]
    for s in range(2):
        brings[4 + s].wait()
        for half in range(2):
            at = 384 * half
            total = jnp.zeros((384, WIDTH), F32)
            for d in range(4):
                row = pl.multiple_of(((place + d) & 3) * WIDTH, WIDTH)
                total = total + jnp.dot(
                    xs[d, at : at + 384, :],
                    ws[s, pl.ds(row, WIDTH), :],
                    preferred_element_type=F32,
                )
            outs[s][at : at + 384, :] = total.astype(outs[s].dtype)


def ready_kernel(p0_ref, p1_ref, p2_ref, p3_ref, base_ref):
    base = p0_ref[...]
    for part_ref in (p1_ref, p2_ref, p3_ref):
        base = base + part_ref[...].astype(F32)
    base_ref[...] = base


def final_kernel(dest_ref, base_ref, back_ref, out_ref):
    for b in range(3):
        lo = 256 * b
        at = lax.broadcasted_iota(I32, (256, BUCKETS), 1)
        pick = (at == dest_ref[lo : lo + 256, :]).astype(F32).astype(BF)
        rows = jnp.dot(pick, back_ref[...], preferred_element_type=F32)
        out_ref[lo : lo + 256, :] = (base_ref[lo : lo + 256, :] + SCALE * rows).astype(BF)


def exchange(x, axis):
    return lax.all_to_all(x, axis, split_axis=0, concat_axis=0, tiled=True)


def sibling(x):
    return lax.ppermute(x, "core", [(0, 1), (1, 0)])


def scalar():
    return pl.BlockSpec(memory_space=pltpu.SMEM)


def hbm(n):
    return [pl.BlockSpec(memory_space=pltpu.HBM)] * n


def turn(x, axis, step):
    return lax.ppermute(x, axis, [(i, (i + step) % 4) for i in range(4)])


def body(tokens, weight, a_pool, b_pool, row_adapter_index, adapter_pool_slot):
    tensor = ("y", "x")
    y = lax.axis_index("y")
    core = lax.axis_index("core").astype(I32).reshape(1)
    payload, dest = pl.pallas_call(
        pack_kernel,
        out_shape=(
            jax.ShapeDtypeStruct((CHIPS, PAY, 128), BF),
            jax.ShapeDtypeStruct((1, ROWS), I32),
        ),
        in_specs=vmem(1) + hbm(1),
        out_specs=tuple(hbm(1) + vmem(1)),
        scratch_shapes=[
            pltpu.VMEM((ROWS, WIDTH), BF),
            pltpu.VMEM((CHIPS, PAY, 128), BF),
            pltpu.SemaphoreType.DMA((1,)),
            pltpu.SemaphoreType.DMA((8,)),
        ],
        compiler_params=params(),
        name="pack",
    )(jnp.concatenate([row_adapter_index, adapter_pool_slot]).reshape(1, -1), tokens)
    tokens, weight, a_pool, b_pool, payload = lax.optimization_barrier(
        (tokens, weight, a_pool, b_pool, payload)
    )
    a_own = a_pool.reshape(HELD * RANK, WIDTH)
    b_own = b_pool.reshape(HELD * RANK, WIDTH)
    a_other, b_other = sibling(a_own), sibling(b_own)
    arrived = exchange(payload, "z")
    xs = [tokens] + [turn(tokens, "x", -d) for d in range(1, 4)]
    ws = []
    for s in range(4):
        mine = lax.dynamic_slice(weight, (((y - s) % 4) * 4 * WIDTH, 0), (4 * WIDTH, WIDTH))
        ws.append(turn(mine, "y", -s) if s else mine)
    place = lax.axis_index("x").astype(I32).reshape(1)

    def base_parts(first):
        return pl.pallas_call(
            base_kernel,
            out_shape=tuple(
                jax.ShapeDtypeStruct((ROWS, WIDTH), BF if s else F32) for s in (first, first + 1)
            ),
            in_specs=[scalar()] + hbm(6),
            out_specs=tuple(vmem(2)),
            scratch_shapes=[
                pltpu.VMEM((4, ROWS, WIDTH), BF),
                pltpu.VMEM((2, 4 * WIDTH, WIDTH), BF),
                pltpu.SemaphoreType.DMA((6,)),
            ],
            compiler_params=params(),
            cost_estimate=pl.CostEstimate(
                flops=2 * ROWS * 8 * WIDTH * WIDTH, bytes_accessed=4 * 2**20, transcendentals=0
            ),
            name="base",
        )(place, *xs, ws[first], ws[first + 1])

    partial, ids = pl.pallas_call(
        shrink_kernel,
        out_shape=(
            jax.ShapeDtypeStruct((TENSOR, RANK, 128), BF),
            jax.ShapeDtypeStruct((TENSOR, 8, 128), F32),
        ),
        in_specs=[scalar()] + vmem(1) + hbm(2),
        out_specs=tuple(vmem(2)),
        scratch_shapes=[pltpu.VMEM((2, HELD * RANK, WIDTH), BF), pltpu.SemaphoreType.DMA((2,))],
        compiler_params=params(),
        name="shrink",
    )(core, arrived, a_own, a_other)
    gathered, p0, p1 = lax.optimization_barrier((exchange(partial, tensor), *base_parts(0)))
    summed = pl.pallas_call(
        sum_kernel,
        out_shape=jax.ShapeDtypeStruct((TENSOR, RANK, 128), BF),
        in_specs=vmem(1),
        out_specs=pl.BlockSpec(memory_space=pltpu.VMEM),
        compiler_params=params(),
        name="total",
    )(gathered)
    shrunk = exchange(summed, tensor)
    marks = pl.pallas_call(
        marks_kernel,
        out_shape=jax.ShapeDtypeStruct((TENSOR, 128, 128), BF),
        in_specs=vmem(1) + hbm(1),
        out_specs=pl.BlockSpec(memory_space=pltpu.VMEM),
        compiler_params=params(),
        name="marks",
    )(ids, b_own)
    expanded = pl.pallas_call(
        expand_kernel,
        out_shape=jax.ShapeDtypeStruct((CHIPS, 2, PAIR, WIDTH), BF),
        in_specs=[scalar()] + vmem(3) + hbm(1),
        out_specs=pl.BlockSpec(memory_space=pltpu.HBM),
        scratch_shapes=[
            pltpu.VMEM((HELD * RANK, WIDTH), BF),
            pltpu.VMEM((2, CHIPS, PAIR, WIDTH), BF),
            pltpu.SemaphoreType.DMA((1,)),
            pltpu.SemaphoreType.DMA((8,)),
        ],
        compiler_params=params(),
        name="expand",
    )(core, shrunk, marks, b_own, b_other)
    p0, p1, p2, p3, expanded = lax.optimization_barrier((p0, p1, *base_parts(2), expanded))
    back = exchange(expanded, "z").reshape(BUCKETS, WIDTH)
    sums = [turn(p, "y", s) for s, p in ((1, p1), (2, p2), (3, p3))]
    base = pl.pallas_call(
        ready_kernel,
        out_shape=jax.ShapeDtypeStruct((ROWS, WIDTH), F32),
        in_specs=vmem(4),
        out_specs=pl.BlockSpec(memory_space=pltpu.VMEM),
        compiler_params=params(),
        name="ready",
    )(p0, *sums)
    return pl.pallas_call(
        final_kernel,
        out_shape=jax.ShapeDtypeStruct((ROWS, WIDTH), BF),
        in_specs=vmem(3),
        out_specs=pl.BlockSpec(memory_space=pltpu.VMEM),
        compiler_params=params(),
        name="final",
    )(dest.reshape(ROWS, 1), base, back)


def solution(mesh):
    fine = Mesh(mesh.devices.reshape(CHIPS, 2, 4, 4), ("z", "core", "y", "x"))
    group = ("z", "core")
    tensor = ("y", "x")
    in_specs = (
        P(group, tensor),
        P(None, tensor),
        P(group, None, tensor),
        P(group, None, tensor),
        P(group),
        P(),
    )
    return jax.shard_map(
        body, mesh=fine, in_specs=in_specs, out_specs=P(group, tensor), check_vma=False
    )
```

```python
import jax
import jax.numpy as jnp
from jax import lax
from jax.experimental import pallas as pl
from jax.experimental.pallas import tpu as pltpu
from jax.sharding import Mesh, PartitionSpec as P

RANK = 64
SLOTS = 4
RPA = 16
PAIR = SLOTS * RPA
GROUPS = 32
HELD = 32
TENSOR = 16
ROWS = 768
WIDTH = 256
BUCKETS = GROUPS * PAIR
CHIPS = 16
PAY = 264
SCALE = 2.0

BF = jnp.bfloat16
F32 = jnp.float32
I32 = jnp.int32
NT = (((1,), (1,)), ((), ()))


def params():
    return pltpu.CompilerParams(vmem_limit_bytes=40 * 1024 * 1024)


def vmem(n):
    return [pl.BlockSpec(memory_space=pltpu.VMEM)] * n


def across(row):
    return jnp.broadcast_to(row, (128, ROWS)).T[:, 0:1]


def pack_kernel(table_ref, tokens_hbm, pay_hbm, dest_ref, tokens_ref, pay_ref, sem, out_sem):
    bring = pltpu.make_async_copy(tokens_hbm, tokens_ref, sem.at[0])
    bring.start()
    adapters = table_ref.shape[1] - ROWS
    index = table_ref[:, 0:ROWS]
    table = table_ref[:, ROWS:]
    line = lax.broadcasted_iota(I32, (8, adapters), 0)
    table = jnp.where(line == 0, table >> 5, table & 31).astype(F32).astype(BF)
    named = lax.broadcasted_iota(I32, (adapters, ROWS), 0) == index
    found = jnp.dot(table, named.astype(F32).astype(BF), preferred_element_type=F32)
    holder, local = found[0:1], found[1:2]
    pool_row = holder * HELD + local
    pool_col = across(pool_row)
    shape = (ROWS, ROWS)
    before = lax.broadcasted_iota(I32, shape, 0) < lax.broadcasted_iota(I32, shape, 1)
    same = (pool_col == pool_row) & before
    place = jnp.sum(same.astype(F32), axis=0, keepdims=True)
    first_col = jnp.where(across(place) == 0, pool_col, -1.0)
    lower = (first_col >= holder * HELD) & (first_col < pool_row)
    rank = jnp.sum(lower.astype(F32), axis=0, keepdims=True)
    dest = ((holder * SLOTS + rank) * RPA + place).astype(I32)
    dest_ref[...] = dest
    line = lax.broadcasted_iota(I32, (8 * CHIPS, ROWS), 0) >> 2
    to = (line == holder.astype(I32)).astype(F32).astype(BF)
    lane_slot = (lax.broadcasted_iota(I32, (128, ROWS), 0) & (PAIR - 1)) >> 4
    value = jnp.where((lane_slot == rank.astype(I32)) & (place == 0), local, 0.0).astype(BF)
    ids = lax.dot_general(to, value, NT, preferred_element_type=F32)
    for z in range(CHIPS):
        pay_ref[z, 256:264, :] = ids[8 * z : 8 * z + 8, :].astype(BF)
    bring.wait()
    sends = []
    for b in range(8):
        at = lax.broadcasted_iota(I32, (256, ROWS), 0) + b * 256
        pick = (at == dest).astype(F32).astype(BF)
        rows = jnp.dot(pick, tokens_ref[...], preferred_element_type=F32).astype(BF)
        for j in range(2):
            for c in range(2):
                at = 128 * j + 64 * c
                pay_ref[2 * b + j, 128 * c : 128 * c + 64, :] = rows[at : at + 64, 0:128]
                pay_ref[2 * b + j, 128 * c + 64 : 128 * c + 128, :] = rows[at : at + 64, 128:256]
        two = pl.ds(2 * b, 2)
        sends.append(pltpu.make_async_copy(pay_ref.at[two], pay_hbm.at[two], out_sem.at[b]))
        sends[-1].start()
    for send in sends:
        send.wait()


def shrink_kernel(core_ref, pay_ref, own_hbm, other_hbm, out_ref, ids_ref, pools, sem):
    core = core_ref[0]
    brings = [
        pltpu.make_async_copy(pool, pools.at[i], sem.at[i])
        for i, pool in enumerate((own_hbm, other_hbm))
    ]
    for bring in brings:
        bring.start()
    low = lax.broadcasted_iota(I32, (8, 128), 1) < PAIR
    for i, c in enumerate((core, 1 - core)):
        brings[i].wait()
        at = pl.multiple_of(128 * c, 128)
        for b in range(4):
            parts = []
            marks = []
            for j in range(4):
                z = 4 * b + j
                both = pay_ref[z, pl.ds(at, 128), :]
                parts.append(jnp.concatenate([both[0:64], both[64:128]], axis=1))
            for j in range(2):
                z = 4 * b + 2 * j
                both = jnp.where(
                    low, pay_ref[z, 256:264, :].astype(F32), pay_ref[z + 1, 256:264, :].astype(F32)
                )
                mark = jnp.where(c == 0, both[0:1, :], both[4:5, :])
                ids_ref[8 * c + 2 * b + j] = jnp.broadcast_to(mark, (8, 128))
                marks.append(mark)
            rows = jnp.concatenate(parts, axis=0)
            mark = jnp.broadcast_to(jnp.concatenate(marks, axis=1), (RANK, 256))
            total = jnp.zeros((RANK, 256), F32)
            for q in range(8):
                prod = lax.dot_general(
                    pools[i, 256 * q : 256 * q + 256, :], rows, NT, preferred_element_type=F32
                )
                for a in range(4):
                    total = jnp.where(mark == 4 * q + a, prod[64 * a : 64 * a + 64], total)
            out_ref[8 * c + 2 * b] = total[:, 0:128].astype(BF)
            out_ref[8 * c + 2 * b + 1] = total[:, 128:256].astype(BF)


def sum_kernel(p_ref, out_ref):
    total = p_ref[0].astype(F32)
    for t in range(1, TENSOR):
        total = total + p_ref[t].astype(F32)
    mine = total.astype(BF)
    for t in range(TENSOR):
        out_ref[t] = mine


def marks_kernel(ids_ref, pool_hbm, out_ref):
    high = (lax.broadcasted_iota(I32, (128, 128), 1) >= RANK).astype(F32)
    for t in range(TENSOR):
        column = jnp.broadcast_to(ids_ref[t][0:1], (128, 128)).T
        out_ref[t] = (column - high).astype(BF)


def expand_kernel(
    core_ref, s_ref, marks_ref, own_ref, other_hbm, out_hbm, other_ref, rows_ref, sem, out_sem
):
    core = core_ref[0]
    bring = pltpu.make_async_copy(other_hbm, other_ref, sem.at[0])
    bring.start()
    sends = []
    for i, (pool_ref, c) in enumerate(((own_ref, core), (other_ref, 1 - core))):
        if i:
            bring.wait()
        for b in range(4):
            at = 8 * c + 2 * b
            s, mark = [], []
            for k in range(2):
                one = s_ref[at + k].astype(F32)
                s.append(jnp.concatenate([one, one], axis=0).T.astype(BF))
                mark.append(marks_ref[at + k])
            s, mark = jnp.concatenate(s, axis=0), jnp.concatenate(mark, axis=0)
            m = jnp.concatenate(
                [
                    jnp.where(mark == jnp.asarray(2 * j, BF), s, jnp.zeros_like(s))
                    for j in range(HELD // 2)
                ],
                axis=1,
            )
            e = jnp.dot(m, pool_ref[...], preferred_element_type=F32)
            part = pl.ds(4 * b, 4)
            rows_ref[i, part] = e.astype(BF).reshape(4, PAIR, WIDTH)
            sends.append(
                pltpu.make_async_copy(
                    rows_ref.at[i, part], out_hbm.at[part, c], out_sem.at[4 * i + b]
                )
            )
            sends[-1].start()
    for send in sends:
        send.wait()


def base_kernel(place_ref, *refs):
    outs, (xs, ws, sem) = refs[6:8], refs[8:11]
    brings = [
        pltpu.make_async_copy(refs[i], xs.at[i] if i < 4 else ws.at[i - 4], sem.at[i])
        for i in range(6)
    ]
    for bring in brings:
        bring.start()
    for bring in brings[0:4]:
        bring.wait()
    place = place_ref[0]
    for s in range(2):
        brings[4 + s].wait()
        for half in range(2):
            at = 384 * half
            total = jnp.zeros((384, WIDTH), F32)
            for d in range(4):
                row = pl.multiple_of(((place + d) & 3) * WIDTH, WIDTH)
                total = total + jnp.dot(
                    xs[d, at : at + 384, :],
                    ws[s, pl.ds(row, WIDTH), :],
                    preferred_element_type=F32,
                )
            outs[s][at : at + 384, :] = total.astype(outs[s].dtype)


def ready_kernel(p0_ref, p1_ref, p2_ref, p3_ref, base_ref):
    base = p0_ref[...]
    for part_ref in (p1_ref, p2_ref, p3_ref):
        base = base + part_ref[...].astype(F32)
    base_ref[...] = base


def final_kernel(dest_ref, base_ref, back_ref, out_ref):
    for b in range(3):
        lo = 256 * b
        at = lax.broadcasted_iota(I32, (256, BUCKETS), 1)
        pick = (at == dest_ref[lo : lo + 256, :]).astype(F32).astype(BF)
        rows = jnp.dot(pick, back_ref[...], preferred_element_type=F32)
        out_ref[lo : lo + 256, :] = (base_ref[lo : lo + 256, :] + SCALE * rows).astype(BF)


def exchange(x, axis):
    return lax.all_to_all(x, axis, split_axis=0, concat_axis=0, tiled=True)


def sibling(x):
    return lax.ppermute(x, "core", [(0, 1), (1, 0)])


def scalar():
    return pl.BlockSpec(memory_space=pltpu.SMEM)


def hbm(n):
    return [pl.BlockSpec(memory_space=pltpu.HBM)] * n


def turn(x, axis, step):
    return lax.ppermute(x, axis, [(i, (i + step) % 4) for i in range(4)])


def body(tokens, weight, a_pool, b_pool, row_adapter_index, adapter_pool_slot):
    tensor = ("y", "x")
    y = lax.axis_index("y")
    core = lax.axis_index("core").astype(I32).reshape(1)
    payload, dest = pl.pallas_call(
        pack_kernel,
        out_shape=(
            jax.ShapeDtypeStruct((CHIPS, PAY, 128), BF),
            jax.ShapeDtypeStruct((1, ROWS), I32),
        ),
        in_specs=vmem(1) + hbm(1),
        out_specs=tuple(hbm(1) + vmem(1)),
        scratch_shapes=[
            pltpu.VMEM((ROWS, WIDTH), BF),
            pltpu.VMEM((CHIPS, PAY, 128), BF),
            pltpu.SemaphoreType.DMA((1,)),
            pltpu.SemaphoreType.DMA((8,)),
        ],
        compiler_params=params(),
        name="pack",
    )(jnp.concatenate([row_adapter_index, adapter_pool_slot]).reshape(1, -1), tokens)
    tokens, weight, a_pool, b_pool, payload = lax.optimization_barrier(
        (tokens, weight, a_pool, b_pool, payload)
    )
    a_own = a_pool.reshape(HELD * RANK, WIDTH)
    b_own = b_pool.reshape(HELD * RANK, WIDTH)
    a_other, b_other = sibling(a_own), sibling(b_own)
    arrived = exchange(payload, "z")
    xs = [tokens] + [turn(tokens, "x", -d) for d in range(1, 4)]
    ws = []
    for s in range(4):
        mine = lax.dynamic_slice(weight, (((y - s) % 4) * 4 * WIDTH, 0), (4 * WIDTH, WIDTH))
        ws.append(turn(mine, "y", -s) if s else mine)
    arrived, *xs = lax.optimization_barrier((arrived, *xs))
    place = lax.axis_index("x").astype(I32).reshape(1)

    def base_parts(first, xs, ws):
        return pl.pallas_call(
            base_kernel,
            out_shape=tuple(
                jax.ShapeDtypeStruct((ROWS, WIDTH), BF if s else F32) for s in (first, first + 1)
            ),
            in_specs=[scalar()] + hbm(6),
            out_specs=tuple(vmem(2)),
            scratch_shapes=[
                pltpu.VMEM((4, ROWS, WIDTH), BF),
                pltpu.VMEM((2, 4 * WIDTH, WIDTH), BF),
                pltpu.SemaphoreType.DMA((6,)),
            ],
            compiler_params=params(),
            cost_estimate=pl.CostEstimate(
                flops=2 * ROWS * 8 * WIDTH * WIDTH, bytes_accessed=4 * 2**20, transcendentals=0
            ),
            name="base",
        )(place, *xs, ws[first], ws[first + 1])

    partial, ids = pl.pallas_call(
        shrink_kernel,
        out_shape=(
            jax.ShapeDtypeStruct((TENSOR, RANK, 128), BF),
            jax.ShapeDtypeStruct((TENSOR, 8, 128), F32),
        ),
        in_specs=[scalar()] + vmem(1) + hbm(2),
        out_specs=tuple(vmem(2)),
        scratch_shapes=[pltpu.VMEM((2, HELD * RANK, WIDTH), BF), pltpu.SemaphoreType.DMA((2,))],
        compiler_params=params(),
        name="shrink",
    )(core, arrived, a_own, a_other)
    gathered = exchange(partial, tensor)
    summed = pl.pallas_call(
        sum_kernel,
        out_shape=jax.ShapeDtypeStruct((TENSOR, RANK, 128), BF),
        in_specs=vmem(1),
        out_specs=pl.BlockSpec(memory_space=pltpu.VMEM),
        compiler_params=params(),
        name="total",
    )(gathered)
    shrunk = exchange(summed, tensor)
    marks = pl.pallas_call(
        marks_kernel,
        out_shape=jax.ShapeDtypeStruct((TENSOR, 128, 128), BF),
        in_specs=vmem(1) + hbm(1),
        out_specs=pl.BlockSpec(memory_space=pltpu.VMEM),
        compiler_params=params(),
        name="marks",
    )(ids, b_own)
    expanded = pl.pallas_call(
        expand_kernel,
        out_shape=jax.ShapeDtypeStruct((CHIPS, 2, PAIR, WIDTH), BF),
        in_specs=[scalar()] + vmem(3) + hbm(1),
        out_specs=pl.BlockSpec(memory_space=pltpu.HBM),
        scratch_shapes=[
            pltpu.VMEM((HELD * RANK, WIDTH), BF),
            pltpu.VMEM((2, CHIPS, PAIR, WIDTH), BF),
            pltpu.SemaphoreType.DMA((1,)),
            pltpu.SemaphoreType.DMA((8,)),
        ],
        compiler_params=params(),
        name="expand",
    )(core, shrunk, marks, b_own, b_other)
    p0, p1, expanded, xs, ws = lax.optimization_barrier((*base_parts(0, xs, ws), expanded, xs, ws))
    back = exchange(expanded, "z").reshape(BUCKETS, WIDTH)
    p2, p3 = base_parts(2, xs, ws)
    sums = [turn(p, "y", s) for s, p in ((1, p1), (2, p2), (3, p3))]
    base = pl.pallas_call(
        ready_kernel,
        out_shape=jax.ShapeDtypeStruct((ROWS, WIDTH), F32),
        in_specs=vmem(4),
        out_specs=pl.BlockSpec(memory_space=pltpu.VMEM),
        compiler_params=params(),
        name="ready",
    )(p0, *sums)
    return pl.pallas_call(
        final_kernel,
        out_shape=jax.ShapeDtypeStruct((ROWS, WIDTH), BF),
        in_specs=vmem(3),
        out_specs=pl.BlockSpec(memory_space=pltpu.VMEM),
        compiler_params=params(),
        name="final",
    )(dest.reshape(ROWS, 1), base, back)


def solution(mesh):
    fine = Mesh(mesh.devices.reshape(CHIPS, 2, 4, 4), ("z", "core", "y", "x"))
    group = ("z", "core")
    tensor = ("y", "x")
    in_specs = (
        P(group, tensor),
        P(None, tensor),
        P(group, None, tensor),
        P(group, None, tensor),
        P(group),
        P(),
    )
    return jax.shard_map(
        body, mesh=fine, in_specs=in_specs, out_specs=P(group, tensor), check_vma=False
    )
```

```python
import jax
import jax.numpy as jnp
from jax import lax
from jax.experimental import pallas as pl
from jax.experimental.pallas import tpu as pltpu
from jax.sharding import Mesh, PartitionSpec as P

RANK = 64
SLOTS = 4
RPA = 16
PAIR = SLOTS * RPA
GROUPS = 32
HELD = 32
TENSOR = 16
ROWS = 768
WIDTH = 256
BUCKETS = GROUPS * PAIR
CHIPS = 16
PAY = 264
SCALE = 2.0

BF = jnp.bfloat16
F32 = jnp.float32
I32 = jnp.int32
NT = (((1,), (1,)), ((), ()))


def params():
    return pltpu.CompilerParams(vmem_limit_bytes=40 * 1024 * 1024)


def vmem(n):
    return [pl.BlockSpec(memory_space=pltpu.VMEM)] * n


def across(row):
    return jnp.broadcast_to(row, (128, ROWS)).T[:, 0:1]


def pack_kernel(table_ref, tokens_hbm, pay_hbm, dest_ref, tokens_ref, pay_ref, sem, out_sem):
    bring = pltpu.make_async_copy(tokens_hbm, tokens_ref, sem.at[0])
    bring.start()
    adapters = table_ref.shape[1] - ROWS
    index = table_ref[:, 0:ROWS]
    table = table_ref[:, ROWS:]
    line = lax.broadcasted_iota(I32, (8, adapters), 0)
    table = jnp.where(line == 0, table >> 5, table & 31).astype(F32).astype(BF)
    named = lax.broadcasted_iota(I32, (adapters, ROWS), 0) == index
    found = jnp.dot(table, named.astype(F32).astype(BF), preferred_element_type=F32)
    holder, local = found[0:1], found[1:2]
    pool_row = holder * HELD + local
    pool_col = across(pool_row)
    shape = (ROWS, ROWS)
    before = lax.broadcasted_iota(I32, shape, 0) < lax.broadcasted_iota(I32, shape, 1)
    same = (pool_col == pool_row) & before
    place = jnp.sum(same.astype(F32), axis=0, keepdims=True)
    first_col = jnp.where(across(place) == 0, pool_col, -1.0)
    lower = (first_col >= holder * HELD) & (first_col < pool_row)
    rank = jnp.sum(lower.astype(F32), axis=0, keepdims=True)
    dest = ((holder * SLOTS + rank) * RPA + place).astype(I32)
    dest_ref[...] = dest
    line = lax.broadcasted_iota(I32, (8 * CHIPS, ROWS), 0) >> 2
    to = (line == holder.astype(I32)).astype(F32).astype(BF)
    lane_slot = (lax.broadcasted_iota(I32, (128, ROWS), 0) & (PAIR - 1)) >> 4
    value = jnp.where((lane_slot == rank.astype(I32)) & (place == 0), local, 0.0).astype(BF)
    ids = lax.dot_general(to, value, NT, preferred_element_type=F32)
    for z in range(CHIPS):
        pay_ref[z, 256:264, :] = ids[8 * z : 8 * z + 8, :].astype(BF)
    bring.wait()
    sends = []
    for b in range(8):
        at = lax.broadcasted_iota(I32, (256, ROWS), 0) + b * 256
        pick = (at == dest).astype(F32).astype(BF)
        rows = jnp.dot(pick, tokens_ref[...], preferred_element_type=F32).astype(BF)
        for j in range(2):
            for c in range(2):
                at = 128 * j + 64 * c
                pay_ref[2 * b + j, 128 * c : 128 * c + 64, :] = rows[at : at + 64, 0:128]
                pay_ref[2 * b + j, 128 * c + 64 : 128 * c + 128, :] = rows[at : at + 64, 128:256]
        two = pl.ds(2 * b, 2)
        sends.append(pltpu.make_async_copy(pay_ref.at[two], pay_hbm.at[two], out_sem.at[b]))
        sends[-1].start()
    for send in sends:
        send.wait()


def shrink_kernel(core_ref, pay_ref, own_hbm, other_hbm, out_ref, ids_ref, pools, sem):
    core = core_ref[0]
    brings = [
        pltpu.make_async_copy(pool, pools.at[i], sem.at[i])
        for i, pool in enumerate((own_hbm, other_hbm))
    ]
    for bring in brings:
        bring.start()
    low = lax.broadcasted_iota(I32, (8, 128), 1) < PAIR
    for i, c in enumerate((core, 1 - core)):
        brings[i].wait()
        at = pl.multiple_of(128 * c, 128)
        for b in range(4):
            parts = []
            marks = []
            for j in range(4):
                z = 4 * b + j
                both = pay_ref[z, pl.ds(at, 128), :]
                parts.append(jnp.concatenate([both[0:64], both[64:128]], axis=1))
            for j in range(2):
                z = 4 * b + 2 * j
                both = jnp.where(
                    low, pay_ref[z, 256:264, :].astype(F32), pay_ref[z + 1, 256:264, :].astype(F32)
                )
                mark = jnp.where(c == 0, both[0:1, :], both[4:5, :])
                ids_ref[pl.ds(8 * c + 2 * b + j, 1), :] = mark.astype(I32)
                marks.append(mark)
            rows = jnp.concatenate(parts, axis=0)
            mark = jnp.broadcast_to(jnp.concatenate(marks, axis=1), (RANK, 256))
            total = jnp.zeros((RANK, 256), F32)
            for q in range(8):
                prod = lax.dot_general(
                    pools[i, 256 * q : 256 * q + 256, :], rows, NT, preferred_element_type=F32
                )
                for a in range(4):
                    total = jnp.where(mark == 4 * q + a, prod[64 * a : 64 * a + 64], total)
            out_ref[8 * c + 2 * b] = total[:, 0:128].astype(BF)
            out_ref[8 * c + 2 * b + 1] = total[:, 128:256].astype(BF)


def sum_kernel(p_ref, pool_hbm, out_ref):
    total = p_ref[0].astype(F32)
    for t in range(1, TENSOR):
        total = total + p_ref[t].astype(F32)
    mine = total.astype(BF)
    for t in range(TENSOR):
        out_ref[t] = mine


def expand_kernel(
    core_ref, slot_ref, s_ref, own_ref, other_hbm, out_hbm, other_ref, rows_ref, sem, out_sem
):
    core = core_ref[0]
    bring = pltpu.make_async_copy(other_hbm, other_ref, sem.at[0])
    bring.start()
    place = (lax.broadcasted_iota(I32, (128, 256), 0) & (PAIR - 1)) >> 4
    mine = place == lax.broadcasted_iota(I32, (128, 256), 1) >> 6
    sends = []
    for i, (pool_ref, c) in enumerate(((own_ref, core), (other_ref, 1 - core))):
        if i:
            bring.wait()
        for b in range(8):
            at = 8 * c + b
            s = s_ref[at].astype(F32)
            s = jnp.concatenate([s, s], axis=0).T
            s = jnp.where(mine, jnp.concatenate([s, s], axis=1), 0.0).astype(BF)
            for k in range(2):
                named = []
                for q in range(SLOTS):
                    row = pl.multiple_of(slot_ref[at, PAIR * k + RPA * q] * RANK, RANK)
                    named.append(pool_ref[pl.ds(row, RANK), :])
                factors = jnp.concatenate(named, axis=0)
                e = jnp.dot(s[64 * k : 64 * k + 64], factors, preferred_element_type=F32)
                rows_ref[i, 2 * b + k] = e.astype(BF)
            if b % 2:
                part = pl.ds(2 * b - 2, 4)
                sends.append(
                    pltpu.make_async_copy(
                        rows_ref.at[i, part], out_hbm.at[part, c], out_sem.at[4 * i + b // 2]
                    )
                )
                sends[-1].start()
    for send in sends:
        send.wait()


def base_kernel(place_ref, *refs):
    outs, (xs, ws, sem) = refs[8:12], refs[12:15]
    brings = [
        pltpu.make_async_copy(refs[i], xs.at[i] if i < 4 else ws.at[i - 4], sem.at[i])
        for i in range(8)
    ]
    for i in (0, 1, 2, 3, 4, 5, 6, 7):
        brings[i].start()
    for bring in brings[0:4]:
        bring.wait()
    place = place_ref[0]
    for s in range(4):
        brings[4 + s].wait()
        for half in range(2):
            at = 384 * half
            total = jnp.zeros((384, WIDTH), F32)
            for d in range(4):
                row = pl.multiple_of(((place + d) & 3) * WIDTH, WIDTH)
                total = total + jnp.dot(
                    xs[d, at : at + 384, :],
                    ws[s, pl.ds(row, WIDTH), :],
                    preferred_element_type=F32,
                )
            outs[s][at : at + 384, :] = total.astype(outs[s].dtype)


def ready_kernel(p0_ref, p1_ref, p2_ref, p3_ref, base_ref):
    base = p0_ref[...]
    for part_ref in (p1_ref, p2_ref, p3_ref):
        base = base + part_ref[...].astype(F32)
    base_ref[...] = base


def final_kernel(dest_ref, base_ref, back_ref, out_ref):
    for b in range(3):
        lo = 256 * b
        at = lax.broadcasted_iota(I32, (256, BUCKETS), 1)
        pick = (at == dest_ref[lo : lo + 256, :]).astype(F32).astype(BF)
        rows = jnp.dot(pick, back_ref[...], preferred_element_type=F32)
        out_ref[lo : lo + 256, :] = (base_ref[lo : lo + 256, :] + SCALE * rows).astype(BF)


def exchange(x, axis):
    return lax.all_to_all(x, axis, split_axis=0, concat_axis=0, tiled=True)


def sibling(x):
    return lax.ppermute(x, "core", [(0, 1), (1, 0)])


def scalar():
    return pl.BlockSpec(memory_space=pltpu.SMEM)


def hbm(n):
    return [pl.BlockSpec(memory_space=pltpu.HBM)] * n


def turn(x, axis, step):
    return lax.ppermute(x, axis, [(i, (i + step) % 4) for i in range(4)])


def body(tokens, weight, a_pool, b_pool, row_adapter_index, adapter_pool_slot):
    tensor = ("y", "x")
    y = lax.axis_index("y")
    core = lax.axis_index("core").astype(I32).reshape(1)
    payload, dest = pl.pallas_call(
        pack_kernel,
        out_shape=(
            jax.ShapeDtypeStruct((CHIPS, PAY, 128), BF),
            jax.ShapeDtypeStruct((1, ROWS), I32),
        ),
        in_specs=vmem(1) + hbm(1),
        out_specs=tuple(hbm(1) + vmem(1)),
        scratch_shapes=[
            pltpu.VMEM((ROWS, WIDTH), BF),
            pltpu.VMEM((CHIPS, PAY, 128), BF),
            pltpu.SemaphoreType.DMA((1,)),
            pltpu.SemaphoreType.DMA((8,)),
        ],
        compiler_params=params(),
        name="pack",
    )(jnp.concatenate([row_adapter_index, adapter_pool_slot]).reshape(1, -1), tokens)
    tokens, weight, a_pool, b_pool, payload = lax.optimization_barrier(
        (tokens, weight, a_pool, b_pool, payload)
    )
    a_own = a_pool.reshape(HELD * RANK, WIDTH)
    b_own = b_pool.reshape(HELD * RANK, WIDTH)
    a_other, b_other = sibling(a_own), sibling(b_own)
    arrived = exchange(payload, "z")
    xs = [tokens] + [turn(tokens, "x", -d) for d in range(1, 4)]
    ws = []
    for s in range(4):
        mine = lax.dynamic_slice(weight, (((y - s) % 4) * 4 * WIDTH, 0), (4 * WIDTH, WIDTH))
        ws.append(turn(mine, "y", -s) if s else mine)
    parts = pl.pallas_call(
        base_kernel,
        out_shape=tuple(jax.ShapeDtypeStruct((ROWS, WIDTH), BF if s else F32) for s in range(4)),
        in_specs=[scalar()] + hbm(8),
        out_specs=tuple(vmem(4)),
        scratch_shapes=[
            pltpu.VMEM((4, ROWS, WIDTH), BF),
            pltpu.VMEM((4, 4 * WIDTH, WIDTH), BF),
            pltpu.SemaphoreType.DMA((8,)),
        ],
        compiler_params=params(),
        cost_estimate=pl.CostEstimate(
            flops=2 * ROWS * 16 * WIDTH * WIDTH, bytes_accessed=6 * 2**20, transcendentals=0
        ),
        name="base",
    )(lax.axis_index("x").astype(I32).reshape(1), *xs, *ws)
    partial, ids = pl.pallas_call(
        shrink_kernel,
        out_shape=(
            jax.ShapeDtypeStruct((TENSOR, RANK, 128), BF),
            jax.ShapeDtypeStruct((TENSOR, 128), I32),
        ),
        in_specs=[scalar()] + vmem(1) + hbm(2),
        out_specs=tuple(vmem(2)),
        scratch_shapes=[pltpu.VMEM((2, HELD * RANK, WIDTH), BF), pltpu.SemaphoreType.DMA((2,))],
        compiler_params=params(),
        name="shrink",
    )(core, arrived, a_own, a_other)
    summed = pl.pallas_call(
        sum_kernel,
        out_shape=jax.ShapeDtypeStruct((TENSOR, RANK, 128), BF),
        in_specs=vmem(1) + hbm(1),
        out_specs=pl.BlockSpec(memory_space=pltpu.VMEM),
        compiler_params=params(),
        name="total",
    )(exchange(partial, tensor), b_own)
    shrunk = exchange(summed, tensor)
    expanded = pl.pallas_call(
        expand_kernel,
        out_shape=jax.ShapeDtypeStruct((CHIPS, 2, PAIR, WIDTH), BF),
        in_specs=[scalar(), scalar()] + vmem(2) + hbm(1),
        out_specs=pl.BlockSpec(memory_space=pltpu.HBM),
        scratch_shapes=[
            pltpu.VMEM((HELD * RANK, WIDTH), BF),
            pltpu.VMEM((2, CHIPS, PAIR, WIDTH), BF),
            pltpu.SemaphoreType.DMA((1,)),
            pltpu.SemaphoreType.DMA((8,)),
        ],
        compiler_params=params(),
        name="expand",
    )(core, ids, shrunk, b_own, b_other)
    p0, p1, p2, p3, expanded = lax.optimization_barrier((*parts, expanded))
    back = exchange(expanded, "z").reshape(BUCKETS, WIDTH)
    sums = [turn(p, "y", s) for s, p in ((1, p1), (2, p2), (3, p3))]
    base = pl.pallas_call(
        ready_kernel,
        out_shape=jax.ShapeDtypeStruct((ROWS, WIDTH), F32),
        in_specs=vmem(4),
        out_specs=pl.BlockSpec(memory_space=pltpu.VMEM),
        compiler_params=params(),
        name="ready",
    )(p0, *sums)
    return pl.pallas_call(
        final_kernel,
        out_shape=jax.ShapeDtypeStruct((ROWS, WIDTH), BF),
        in_specs=vmem(3),
        out_specs=pl.BlockSpec(memory_space=pltpu.VMEM),
        compiler_params=params(),
        name="final",
    )(dest.reshape(ROWS, 1), base, back)


def solution(mesh):
    fine = Mesh(mesh.devices.reshape(CHIPS, 2, 4, 4), ("z", "core", "y", "x"))
    group = ("z", "core")
    tensor = ("y", "x")
    in_specs = (
        P(group, tensor),
        P(None, tensor),
        P(group, None, tensor),
        P(group, None, tensor),
        P(group),
        P(),
    )
    return jax.shard_map(
        body, mesh=fine, in_specs=in_specs, out_specs=P(group, tensor), check_vma=False
    )
```

```python
import jax
import jax.numpy as jnp
from jax import lax
from jax.experimental import pallas as pl
from jax.experimental.pallas import tpu as pltpu
from jax.sharding import Mesh, PartitionSpec as P

RANK = 64
SLOTS = 4
RPA = 16
PAIR = SLOTS * RPA
GROUPS = 32
HELD = 32
TENSOR = 16
ROWS = 768
WIDTH = 256
BUCKETS = GROUPS * PAIR
CHIPS = 16
PAY = 264
SCALE = 2.0

BF = jnp.bfloat16
F32 = jnp.float32
I32 = jnp.int32
NT = (((1,), (1,)), ((), ()))


def params():
    return pltpu.CompilerParams(vmem_limit_bytes=40 * 1024 * 1024)


def vmem(n):
    return [pl.BlockSpec(memory_space=pltpu.VMEM)] * n


def across(row):
    return jnp.broadcast_to(row, (128, ROWS)).T[:, 0:1]


def pack_kernel(table_ref, tokens_hbm, pay_hbm, dest_ref, tokens_ref, pay_ref, sem, out_sem):
    bring = pltpu.make_async_copy(tokens_hbm, tokens_ref, sem.at[0])
    bring.start()
    adapters = table_ref.shape[1] - ROWS
    index = table_ref[:, 0:ROWS]
    table = table_ref[:, ROWS:]
    line = lax.broadcasted_iota(I32, (8, adapters), 0)
    table = jnp.where(line == 0, table >> 5, table & 31).astype(F32).astype(BF)
    named = lax.broadcasted_iota(I32, (adapters, ROWS), 0) == index
    found = jnp.dot(table, named.astype(F32).astype(BF), preferred_element_type=F32)
    holder, local = found[0:1], found[1:2]
    pool_row = holder * HELD + local
    pool_col = across(pool_row)
    shape = (ROWS, ROWS)
    before = lax.broadcasted_iota(I32, shape, 0) < lax.broadcasted_iota(I32, shape, 1)
    same = (pool_col == pool_row) & before
    place = jnp.sum(same.astype(F32), axis=0, keepdims=True)
    first_col = jnp.where(across(place) == 0, pool_col, -1.0)
    lower = (first_col >= holder * HELD) & (first_col < pool_row)
    rank = jnp.sum(lower.astype(F32), axis=0, keepdims=True)
    dest = ((holder * SLOTS + rank) * RPA + place).astype(I32)
    dest_ref[...] = dest
    line = lax.broadcasted_iota(I32, (8 * CHIPS, ROWS), 0) >> 2
    to = (line == holder.astype(I32)).astype(F32).astype(BF)
    lane_slot = (lax.broadcasted_iota(I32, (128, ROWS), 0) & (PAIR - 1)) >> 4
    value = jnp.where((lane_slot == rank.astype(I32)) & (place == 0), local, 0.0).astype(BF)
    ids = lax.dot_general(to, value, NT, preferred_element_type=F32)
    for z in range(CHIPS):
        pay_ref[z, 256:264, :] = ids[8 * z : 8 * z + 8, :].astype(BF)
    bring.wait()
    sends = []
    for b in range(8):
        at = lax.broadcasted_iota(I32, (256, ROWS), 0) + b * 256
        pick = (at == dest).astype(F32).astype(BF)
        rows = jnp.dot(pick, tokens_ref[...], preferred_element_type=F32).astype(BF)
        for j in range(2):
            for c in range(2):
                at = 128 * j + 64 * c
                pay_ref[2 * b + j, 128 * c : 128 * c + 64, :] = rows[at : at + 64, 0:128]
                pay_ref[2 * b + j, 128 * c + 64 : 128 * c + 128, :] = rows[at : at + 64, 128:256]
        two = pl.ds(2 * b, 2)
        sends.append(pltpu.make_async_copy(pay_ref.at[two], pay_hbm.at[two], out_sem.at[b]))
        sends[-1].start()
    for send in sends:
        send.wait()


def shrink_kernel(core_ref, pay_ref, own_hbm, other_hbm, out_ref, ids_ref, pools, sem):
    core = core_ref[0]
    brings = [
        pltpu.make_async_copy(pool, pools.at[i], sem.at[i])
        for i, pool in enumerate((own_hbm, other_hbm))
    ]
    for bring in brings:
        bring.start()
    low = lax.broadcasted_iota(I32, (8, 128), 1) < PAIR
    for i, c in enumerate((core, 1 - core)):
        brings[i].wait()
        at = pl.multiple_of(128 * c, 128)
        for b in range(4):
            parts = []
            marks = []
            for j in range(4):
                z = 4 * b + j
                both = pay_ref[z, pl.ds(at, 128), :]
                parts.append(jnp.concatenate([both[0:64], both[64:128]], axis=1))
            for j in range(2):
                z = 4 * b + 2 * j
                both = jnp.where(
                    low, pay_ref[z, 256:264, :].astype(F32), pay_ref[z + 1, 256:264, :].astype(F32)
                )
                mark = jnp.where(c == 0, both[0:1, :], both[4:5, :])
                ids_ref[pl.ds(8 * c + 2 * b + j, 1), :] = mark.astype(I32)
                marks.append(mark)
            rows = jnp.concatenate(parts, axis=0)
            mark = jnp.broadcast_to(jnp.concatenate(marks, axis=1), (RANK, 256))
            total = jnp.zeros((RANK, 256), F32)
            for q in range(8):
                prod = lax.dot_general(
                    pools[i, 256 * q : 256 * q + 256, :], rows, NT, preferred_element_type=F32
                )
                for a in range(4):
                    total = jnp.where(mark == 4 * q + a, prod[64 * a : 64 * a + 64], total)
            out_ref[8 * c + 2 * b] = total[:, 0:128].astype(BF)
            out_ref[8 * c + 2 * b + 1] = total[:, 128:256].astype(BF)


def sum_kernel(p_ref, pool_hbm, out_ref):
    total = p_ref[0].astype(F32)
    for t in range(1, TENSOR):
        total = total + p_ref[t].astype(F32)
    mine = total.astype(BF)
    for t in range(TENSOR):
        out_ref[t] = mine


def expand_kernel(
    core_ref, ids_ref, s_ref, own_ref, other_hbm, out_hbm, slot_ref, mine_ref, other_ref, rows_ref, sem, out_sem
):
    core = core_ref[0]
    slots = pltpu.make_async_copy(ids_ref, slot_ref, sem.at[4])
    slots.start()
    quarters = [pl.ds(512 * k, 512) for k in range(4)]
    brings = [
        pltpu.make_async_copy(other_hbm.at[part], other_ref.at[part], sem.at[k])
        for k, part in enumerate(quarters)
    ]
    for bring in brings:
        bring.start()
    place = (lax.broadcasted_iota(I32, (128, 256), 0) & (PAIR - 1)) >> 4
    mine = place == lax.broadcasted_iota(I32, (128, 256), 1) >> 6
    for t in range(TENSOR):
        s = s_ref[t].astype(F32)
        s = jnp.concatenate([s, s], axis=0).T
        mine_ref[t] = jnp.where(mine, jnp.concatenate([s, s], axis=1), 0.0).astype(BF)
    slots.wait()
    sends = []
    for i, (pool_ref, c) in enumerate(((own_ref, core), (other_ref, 1 - core))):
        if i:
            for bring in brings:
                bring.wait()
        for b in range(8):
            at = 8 * c + b
            s = mine_ref[at]
            for k in range(2):
                named = []
                for q in range(SLOTS):
                    row = pl.multiple_of(slot_ref[at, PAIR * k + RPA * q] * RANK, RANK)
                    named.append(pool_ref[pl.ds(row, RANK), :])
                factors = jnp.concatenate(named, axis=0)
                e = jnp.dot(s[64 * k : 64 * k + 64], factors, preferred_element_type=F32)
                rows_ref[i, 2 * b + k] = e.astype(BF)
            if b % 2:
                part = pl.ds(2 * b - 2, 4)
                sends.append(
                    pltpu.make_async_copy(
                        rows_ref.at[i, part], out_hbm.at[part, c], out_sem.at[4 * i + b // 2]
                    )
                )
                sends[-1].start()
    for send in sends:
        send.wait()


def base_kernel(place_ref, *refs):
    outs, (xs, ws, sem) = refs[8:12], refs[12:15]
    brings = [
        pltpu.make_async_copy(refs[i], xs.at[i] if i < 4 else ws.at[i - 4], sem.at[i])
        for i in range(8)
    ]
    for i in (0, 1, 2, 3, 4, 5, 6, 7):
        brings[i].start()
    for bring in brings[0:4]:
        bring.wait()
    place = place_ref[0]
    for s in range(4):
        brings[4 + s].wait()
        for half in range(2):
            at = 384 * half
            total = jnp.zeros((384, WIDTH), F32)
            for d in range(4):
                row = pl.multiple_of(((place + d) & 3) * WIDTH, WIDTH)
                total = total + jnp.dot(
                    xs[d, at : at + 384, :],
                    ws[s, pl.ds(row, WIDTH), :],
                    preferred_element_type=F32,
                )
            outs[s][at : at + 384, :] = total.astype(outs[s].dtype)


def ready_kernel(p0_ref, p1_ref, p2_ref, p3_ref, base_ref):
    base = p0_ref[...]
    for part_ref in (p1_ref, p2_ref, p3_ref):
        base = base + part_ref[...].astype(F32)
    base_ref[...] = base


def final_kernel(dest_ref, base_ref, back_ref, out_hbm, out_ref, sem):
    sends = []
    for b in range(3):
        lo = 256 * b
        at = lax.broadcasted_iota(I32, (256, BUCKETS), 1)
        pick = (at == dest_ref[lo : lo + 256, :]).astype(F32).astype(BF)
        rows = jnp.dot(pick, back_ref[...], preferred_element_type=F32)
        out_ref[lo : lo + 256, :] = (base_ref[lo : lo + 256, :] + SCALE * rows).astype(BF)
        part = pl.ds(lo, 256)
        sends.append(pltpu.make_async_copy(out_ref.at[part], out_hbm.at[part], sem.at[b]))
        sends[-1].start()
    for send in sends:
        send.wait()


def exchange(x, axis):
    return lax.all_to_all(x, axis, split_axis=0, concat_axis=0, tiled=True)


def sibling(x):
    return lax.ppermute(x, "core", [(0, 1), (1, 0)])


def scalar():
    return pl.BlockSpec(memory_space=pltpu.SMEM)


def hbm(n):
    return [pl.BlockSpec(memory_space=pltpu.HBM)] * n


def turn(x, axis, step):
    return lax.ppermute(x, axis, [(i, (i + step) % 4) for i in range(4)])


def body(tokens, weight, a_pool, b_pool, row_adapter_index, adapter_pool_slot):
    tensor = ("y", "x")
    y = lax.axis_index("y")
    core = lax.axis_index("core").astype(I32).reshape(1)
    payload, dest = pl.pallas_call(
        pack_kernel,
        out_shape=(
            jax.ShapeDtypeStruct((CHIPS, PAY, 128), BF),
            jax.ShapeDtypeStruct((1, ROWS), I32),
        ),
        in_specs=vmem(1) + hbm(1),
        out_specs=tuple(hbm(1) + vmem(1)),
        scratch_shapes=[
            pltpu.VMEM((ROWS, WIDTH), BF),
            pltpu.VMEM((CHIPS, PAY, 128), BF),
            pltpu.SemaphoreType.DMA((1,)),
            pltpu.SemaphoreType.DMA((8,)),
        ],
        compiler_params=params(),
        name="pack",
    )(jnp.concatenate([row_adapter_index, adapter_pool_slot]).reshape(1, -1), tokens)
    tokens, weight, a_pool, b_pool, payload = lax.optimization_barrier(
        (tokens, weight, a_pool, b_pool, payload)
    )
    a_own = a_pool.reshape(HELD * RANK, WIDTH)
    b_own = b_pool.reshape(HELD * RANK, WIDTH)
    a_other, b_other = sibling(a_own), sibling(b_own)
    arrived = exchange(payload, "z")
    xs = [tokens] + [turn(tokens, "x", -d) for d in range(1, 4)]
    ws = []
    for s in range(4):
        mine = lax.dynamic_slice(weight, (((y - s) % 4) * 4 * WIDTH, 0), (4 * WIDTH, WIDTH))
        ws.append(turn(mine, "y", -s) if s else mine)
    parts = pl.pallas_call(
        base_kernel,
        out_shape=tuple(jax.ShapeDtypeStruct((ROWS, WIDTH), BF if s else F32) for s in range(4)),
        in_specs=[scalar()] + hbm(8),
        out_specs=tuple(vmem(4)),
        scratch_shapes=[
            pltpu.VMEM((4, ROWS, WIDTH), BF),
            pltpu.VMEM((4, 4 * WIDTH, WIDTH), BF),
            pltpu.SemaphoreType.DMA((8,)),
        ],
        compiler_params=params(),
        cost_estimate=pl.CostEstimate(
            flops=2 * ROWS * 16 * WIDTH * WIDTH, bytes_accessed=6 * 2**20, transcendentals=0
        ),
        name="base",
    )(lax.axis_index("x").astype(I32).reshape(1), *xs, *ws)
    partial, ids = pl.pallas_call(
        shrink_kernel,
        out_shape=(
            jax.ShapeDtypeStruct((TENSOR, RANK, 128), BF),
            jax.ShapeDtypeStruct((TENSOR, 128), I32),
        ),
        in_specs=[scalar()] + vmem(1) + hbm(2),
        out_specs=tuple(vmem(2)),
        scratch_shapes=[pltpu.VMEM((2, HELD * RANK, WIDTH), BF), pltpu.SemaphoreType.DMA((2,))],
        compiler_params=params(),
        name="shrink",
    )(core, arrived, a_own, a_other)
    summed = pl.pallas_call(
        sum_kernel,
        out_shape=jax.ShapeDtypeStruct((TENSOR, RANK, 128), BF),
        in_specs=vmem(1) + hbm(1),
        out_specs=pl.BlockSpec(memory_space=pltpu.VMEM),
        compiler_params=params(),
        name="total",
    )(exchange(partial, tensor), b_own)
    shrunk = exchange(summed, tensor)
    expanded = pl.pallas_call(
        expand_kernel,
        out_shape=jax.ShapeDtypeStruct((CHIPS, 2, PAIR, WIDTH), BF),
        in_specs=[scalar()] + vmem(3) + hbm(1),
        out_specs=pl.BlockSpec(memory_space=pltpu.HBM),
        scratch_shapes=[
            pltpu.SMEM((TENSOR, 128), I32),
            pltpu.VMEM((TENSOR, 128, 256), BF),
            pltpu.VMEM((HELD * RANK, WIDTH), BF),
            pltpu.VMEM((2, CHIPS, PAIR, WIDTH), BF),
            pltpu.SemaphoreType.DMA((5,)),
            pltpu.SemaphoreType.DMA((8,)),
        ],
        compiler_params=params(),
        name="expand",
    )(core, ids, shrunk, b_own, b_other)
    p0, p1, p2, p3, expanded = lax.optimization_barrier((*parts, expanded))
    back = exchange(expanded, "z").reshape(BUCKETS, WIDTH)
    sums = [turn(p, "y", s) for s, p in ((1, p1), (2, p2), (3, p3))]
    base = pl.pallas_call(
        ready_kernel,
        out_shape=jax.ShapeDtypeStruct((ROWS, WIDTH), F32),
        in_specs=vmem(4),
        out_specs=pl.BlockSpec(memory_space=pltpu.VMEM),
        compiler_params=params(),
        name="ready",
    )(p0, *sums)
    return pl.pallas_call(
        final_kernel,
        out_shape=jax.ShapeDtypeStruct((ROWS, WIDTH), BF),
        in_specs=vmem(3),
        out_specs=pl.BlockSpec(memory_space=pltpu.HBM),
        scratch_shapes=[pltpu.VMEM((ROWS, WIDTH), BF), pltpu.SemaphoreType.DMA((3,))],
        compiler_params=params(),
        name="final",
    )(dest.reshape(ROWS, 1), base, back)


def solution(mesh):
    fine = Mesh(mesh.devices.reshape(CHIPS, 2, 4, 4), ("z", "core", "y", "x"))
    group = ("z", "core")
    tensor = ("y", "x")
    in_specs = (
        P(group, tensor),
        P(None, tensor),
        P(group, None, tensor),
        P(group, None, tensor),
        P(group),
        P(),
    )
    return jax.shard_map(
        body, mesh=fine, in_specs=in_specs, out_specs=P(group, tensor), check_vma=False
    )
```

```python
import jax
import jax.numpy as jnp
from jax import lax
from jax.experimental import pallas as pl
from jax.experimental.pallas import tpu as pltpu
from jax.sharding import Mesh, PartitionSpec as P

RANK = 64
SLOTS = 4
RPA = 16
PAIR = SLOTS * RPA
GROUPS = 32
HELD = 32
TENSOR = 16
ROWS = 768
WIDTH = 256
BUCKETS = GROUPS * PAIR
CHIPS = 16
PAY = 264
SCALE = 2.0

BF = jnp.bfloat16
F32 = jnp.float32
I32 = jnp.int32
NT = (((1,), (1,)), ((), ()))


def params():
    return pltpu.CompilerParams(vmem_limit_bytes=40 * 1024 * 1024)


def vmem(n):
    return [pl.BlockSpec(memory_space=pltpu.VMEM)] * n


def across(row):
    return jnp.broadcast_to(row, (128, ROWS)).T[:, 0:1]


def pack_kernel(table_ref, tokens_hbm, pay_hbm, dest_ref, tokens_ref, pay_ref, sem, out_sem):
    thirds = [pl.ds(256 * k, 256) for k in range(3)]
    brings = [
        pltpu.make_async_copy(tokens_hbm.at[part], tokens_ref.at[part], sem.at[k])
        for k, part in enumerate(thirds)
    ]
    for bring in brings:
        bring.start()
    adapters = table_ref.shape[1] - ROWS
    index = table_ref[:, 0:ROWS]
    table = table_ref[:, ROWS:]
    line = lax.broadcasted_iota(I32, (8, adapters), 0)
    table = jnp.where(line == 0, table >> 5, table & 31).astype(F32).astype(BF)
    named = lax.broadcasted_iota(I32, (adapters, ROWS), 0) == index
    found = jnp.dot(table, named.astype(F32).astype(BF), preferred_element_type=F32)
    holder, local = found[0:1], found[1:2]
    pool_row = holder * HELD + local
    pool_col = across(pool_row)
    shape = (ROWS, ROWS)
    before = lax.broadcasted_iota(I32, shape, 0) < lax.broadcasted_iota(I32, shape, 1)
    same = (pool_col == pool_row) & before
    place = jnp.sum(same.astype(F32), axis=0, keepdims=True)
    first_col = jnp.where(across(place) == 0, pool_col, -1.0)
    lower = (first_col >= holder * HELD) & (first_col < pool_row)
    rank = jnp.sum(lower.astype(F32), axis=0, keepdims=True)
    dest = ((holder * SLOTS + rank) * RPA + place).astype(I32)
    dest_ref[...] = dest
    line = lax.broadcasted_iota(I32, (8 * CHIPS, ROWS), 0) >> 2
    to = (line == holder.astype(I32)).astype(F32).astype(BF)
    lane_slot = (lax.broadcasted_iota(I32, (128, ROWS), 0) & (PAIR - 1)) >> 4
    value = jnp.where((lane_slot == rank.astype(I32)) & (place == 0), local, 0.0).astype(BF)
    ids = lax.dot_general(to, value, NT, preferred_element_type=F32)
    for z in range(CHIPS):
        pay_ref[z, 256:264, :] = ids[8 * z : 8 * z + 8, :].astype(BF)
    for bring in brings:
        bring.wait()
    sends = []
    for b in range(8):
        at = lax.broadcasted_iota(I32, (256, ROWS), 0) + b * 256
        pick = (at == dest).astype(F32).astype(BF)
        rows = jnp.dot(pick, tokens_ref[...], preferred_element_type=F32).astype(BF)
        for j in range(2):
            for c in range(2):
                at = 128 * j + 64 * c
                pay_ref[2 * b + j, 128 * c : 128 * c + 64, :] = rows[at : at + 64, 0:128]
                pay_ref[2 * b + j, 128 * c + 64 : 128 * c + 128, :] = rows[at : at + 64, 128:256]
        two = pl.ds(2 * b, 2)
        sends.append(pltpu.make_async_copy(pay_ref.at[two], pay_hbm.at[two], out_sem.at[b]))
        sends[-1].start()
    for send in sends:
        send.wait()


def shrink_kernel(core_ref, pay_ref, own_hbm, other_hbm, out_ref, ids_ref, pools, sem):
    core = core_ref[0]
    quarters = [pl.ds(512 * k, 512) for k in range(4)]
    brings = [
        [
            pltpu.make_async_copy(pool.at[part], pools.at[i, part], sem.at[4 * i + k])
            for k, part in enumerate(quarters)
        ]
        for i, pool in enumerate((own_hbm, other_hbm))
    ]
    for bring in brings[0] + brings[1]:
        bring.start()
    low = lax.broadcasted_iota(I32, (8, 128), 1) < PAIR
    for i, c in enumerate((core, 1 - core)):
        for bring in brings[i]:
            bring.wait()
        at = pl.multiple_of(128 * c, 128)
        for b in range(4):
            parts = []
            marks = []
            for j in range(4):
                z = 4 * b + j
                both = pay_ref[z, pl.ds(at, 128), :]
                parts.append(jnp.concatenate([both[0:64], both[64:128]], axis=1))
            for j in range(2):
                z = 4 * b + 2 * j
                both = jnp.where(
                    low, pay_ref[z, 256:264, :].astype(F32), pay_ref[z + 1, 256:264, :].astype(F32)
                )
                mark = jnp.where(c == 0, both[0:1, :], both[4:5, :])
                ids_ref[pl.ds(8 * c + 2 * b + j, 1), :] = mark.astype(I32)
                marks.append(mark)
            rows = jnp.concatenate(parts, axis=0)
            mark = jnp.broadcast_to(jnp.concatenate(marks, axis=1), (RANK, 256))
            total = jnp.zeros((RANK, 256), F32)
            for q in range(8):
                prod = lax.dot_general(
                    pools[i, 256 * q : 256 * q + 256, :], rows, NT, preferred_element_type=F32
                )
                for a in range(4):
                    total = jnp.where(mark == 4 * q + a, prod[64 * a : 64 * a + 64], total)
            out_ref[8 * c + 2 * b] = total[:, 0:128].astype(BF)
            out_ref[8 * c + 2 * b + 1] = total[:, 128:256].astype(BF)


def sum_kernel(p_ref, pool_hbm, out_ref):
    total = p_ref[0].astype(F32)
    for t in range(1, TENSOR):
        total = total + p_ref[t].astype(F32)
    mine = total.astype(BF)
    for t in range(TENSOR):
        out_ref[t] = mine


def expand_kernel(
    core_ref, ids_ref, s_ref, own_ref, other_hbm, out_hbm, slot_ref, mine_ref, other_ref, rows_ref, sem, out_sem
):
    core = core_ref[0]
    slots = pltpu.make_async_copy(ids_ref, slot_ref, sem.at[4])
    slots.start()
    quarters = [pl.ds(512 * k, 512) for k in range(4)]
    brings = [
        pltpu.make_async_copy(other_hbm.at[part], other_ref.at[part], sem.at[k])
        for k, part in enumerate(quarters)
    ]
    for bring in brings:
        bring.start()
    place = (lax.broadcasted_iota(I32, (128, 256), 0) & (PAIR - 1)) >> 4
    mine = place == lax.broadcasted_iota(I32, (128, 256), 1) >> 6
    for t in range(TENSOR):
        s = s_ref[t].astype(F32)
        s = jnp.concatenate([s, s], axis=0).T
        mine_ref[t] = jnp.where(mine, jnp.concatenate([s, s], axis=1), 0.0).astype(BF)
    slots.wait()
    sends = []
    for i, (pool_ref, c) in enumerate(((own_ref, core), (other_ref, 1 - core))):
        if i:
            for bring in brings:
                bring.wait()
        for b in range(8):
            at = 8 * c + b
            s = mine_ref[at]
            for k in range(2):
                named = []
                for q in range(SLOTS):
                    row = pl.multiple_of(slot_ref[at, PAIR * k + RPA * q] * RANK, RANK)
                    named.append(pool_ref[pl.ds(row, RANK), :])
                factors = jnp.concatenate(named, axis=0)
                e = jnp.dot(s[64 * k : 64 * k + 64], factors, preferred_element_type=F32)
                rows_ref[i, 2 * b + k] = e.astype(BF)
            if b % 2:
                part = pl.ds(2 * b - 2, 4)
                sends.append(
                    pltpu.make_async_copy(
                        rows_ref.at[i, part], out_hbm.at[part, c], out_sem.at[4 * i + b // 2]
                    )
                )
                sends[-1].start()
    for send in sends:
        send.wait()


def base_kernel(place_ref, *refs):
    outs, (xs, ws, sem) = refs[8:12], refs[12:15]
    brings = [
        pltpu.make_async_copy(refs[i], xs.at[i] if i < 4 else ws.at[i - 4], sem.at[i])
        for i in range(8)
    ]
    for i in (0, 1, 2, 3, 4, 5, 6, 7):
        brings[i].start()
    for bring in brings[0:4]:
        bring.wait()
    place = place_ref[0]
    for s in range(4):
        brings[4 + s].wait()
        for half in range(2):
            at = 384 * half
            total = jnp.zeros((384, WIDTH), F32)
            for d in range(4):
                row = pl.multiple_of(((place + d) & 3) * WIDTH, WIDTH)
                total = total + jnp.dot(
                    xs[d, at : at + 384, :],
                    ws[s, pl.ds(row, WIDTH), :],
                    preferred_element_type=F32,
                )
            outs[s][at : at + 384, :] = total.astype(outs[s].dtype)


def ready_kernel(p0_ref, p1_ref, p2_ref, p3_ref, base_ref):
    base = p0_ref[...]
    for part_ref in (p1_ref, p2_ref, p3_ref):
        base = base + part_ref[...].astype(F32)
    base_ref[...] = base


def final_kernel(dest_ref, base_ref, back_ref, out_hbm, out_ref, sem):
    sends = []
    for b in range(3):
        lo = 256 * b
        at = lax.broadcasted_iota(I32, (256, BUCKETS), 1)
        pick = (at == dest_ref[lo : lo + 256, :]).astype(F32).astype(BF)
        rows = jnp.dot(pick, back_ref[...], preferred_element_type=F32)
        out_ref[lo : lo + 256, :] = (base_ref[lo : lo + 256, :] + SCALE * rows).astype(BF)
        part = pl.ds(lo, 256)
        sends.append(pltpu.make_async_copy(out_ref.at[part], out_hbm.at[part], sem.at[b]))
        sends[-1].start()
    for send in sends:
        send.wait()


def exchange(x, axis):
    return lax.all_to_all(x, axis, split_axis=0, concat_axis=0, tiled=True)


def sibling(x):
    return lax.ppermute(x, "core", [(0, 1), (1, 0)])


def scalar():
    return pl.BlockSpec(memory_space=pltpu.SMEM)


def hbm(n):
    return [pl.BlockSpec(memory_space=pltpu.HBM)] * n


def turn(x, axis, step):
    return lax.ppermute(x, axis, [(i, (i + step) % 4) for i in range(4)])


def body(tokens, weight, a_pool, b_pool, row_adapter_index, adapter_pool_slot):
    tensor = ("y", "x")
    y = lax.axis_index("y")
    core = lax.axis_index("core").astype(I32).reshape(1)
    payload, dest = pl.pallas_call(
        pack_kernel,
        out_shape=(
            jax.ShapeDtypeStruct((CHIPS, PAY, 128), BF),
            jax.ShapeDtypeStruct((1, ROWS), I32),
        ),
        in_specs=vmem(1) + hbm(1),
        out_specs=tuple(hbm(1) + vmem(1)),
        scratch_shapes=[
            pltpu.VMEM((ROWS, WIDTH), BF),
            pltpu.VMEM((CHIPS, PAY, 128), BF),
            pltpu.SemaphoreType.DMA((3,)),
            pltpu.SemaphoreType.DMA((8,)),
        ],
        compiler_params=params(),
        name="pack",
    )(jnp.concatenate([row_adapter_index, adapter_pool_slot]).reshape(1, -1), tokens)
    tokens, weight, a_pool, b_pool, payload = lax.optimization_barrier(
        (tokens, weight, a_pool, b_pool, payload)
    )
    a_own = a_pool.reshape(HELD * RANK, WIDTH)
    b_own = b_pool.reshape(HELD * RANK, WIDTH)
    a_other, b_other = sibling(a_own), sibling(b_own)
    arrived = exchange(payload, "z")
    xs = [tokens] + [turn(tokens, "x", -d) for d in range(1, 4)]
    ws = []
    for s in range(4):
        mine = lax.dynamic_slice(weight, (((y - s) % 4) * 4 * WIDTH, 0), (4 * WIDTH, WIDTH))
        ws.append(turn(mine, "y", -s) if s else mine)
    parts = pl.pallas_call(
        base_kernel,
        out_shape=tuple(jax.ShapeDtypeStruct((ROWS, WIDTH), BF if s else F32) for s in range(4)),
        in_specs=[scalar()] + hbm(8),
        out_specs=tuple(vmem(4)),
        scratch_shapes=[
            pltpu.VMEM((4, ROWS, WIDTH), BF),
            pltpu.VMEM((4, 4 * WIDTH, WIDTH), BF),
            pltpu.SemaphoreType.DMA((8,)),
        ],
        compiler_params=params(),
        cost_estimate=pl.CostEstimate(
            flops=2 * ROWS * 16 * WIDTH * WIDTH, bytes_accessed=6 * 2**20, transcendentals=0
        ),
        name="base",
    )(lax.axis_index("x").astype(I32).reshape(1), *xs, *ws)
    partial, ids = pl.pallas_call(
        shrink_kernel,
        out_shape=(
            jax.ShapeDtypeStruct((TENSOR, RANK, 128), BF),
            jax.ShapeDtypeStruct((TENSOR, 128), I32),
        ),
        in_specs=[scalar()] + vmem(1) + hbm(2),
        out_specs=tuple(vmem(2)),
        scratch_shapes=[pltpu.VMEM((2, HELD * RANK, WIDTH), BF), pltpu.SemaphoreType.DMA((8,))],
        compiler_params=params(),
        name="shrink",
    )(core, arrived, a_own, a_other)
    summed = pl.pallas_call(
        sum_kernel,
        out_shape=jax.ShapeDtypeStruct((TENSOR, RANK, 128), BF),
        in_specs=vmem(1) + hbm(1),
        out_specs=pl.BlockSpec(memory_space=pltpu.VMEM),
        compiler_params=params(),
        name="total",
    )(exchange(partial, tensor), b_own)
    shrunk = exchange(summed, tensor)
    expanded = pl.pallas_call(
        expand_kernel,
        out_shape=jax.ShapeDtypeStruct((CHIPS, 2, PAIR, WIDTH), BF),
        in_specs=[scalar()] + vmem(3) + hbm(1),
        out_specs=pl.BlockSpec(memory_space=pltpu.HBM),
        scratch_shapes=[
            pltpu.SMEM((TENSOR, 128), I32),
            pltpu.VMEM((TENSOR, 128, 256), BF),
            pltpu.VMEM((HELD * RANK, WIDTH), BF),
            pltpu.VMEM((2, CHIPS, PAIR, WIDTH), BF),
            pltpu.SemaphoreType.DMA((5,)),
            pltpu.SemaphoreType.DMA((8,)),
        ],
        compiler_params=params(),
        name="expand",
    )(core, ids, shrunk, b_own, b_other)
    p0, p1, p2, p3, expanded = lax.optimization_barrier((*parts, expanded))
    back = exchange(expanded, "z").reshape(BUCKETS, WIDTH)
    sums = [turn(p, "y", s) for s, p in ((1, p1), (2, p2), (3, p3))]
    base = pl.pallas_call(
        ready_kernel,
        out_shape=jax.ShapeDtypeStruct((ROWS, WIDTH), F32),
        in_specs=vmem(4),
        out_specs=pl.BlockSpec(memory_space=pltpu.VMEM),
        compiler_params=params(),
        name="ready",
    )(p0, *sums)
    return pl.pallas_call(
        final_kernel,
        out_shape=jax.ShapeDtypeStruct((ROWS, WIDTH), BF),
        in_specs=vmem(3),
        out_specs=pl.BlockSpec(memory_space=pltpu.HBM),
        scratch_shapes=[pltpu.VMEM((ROWS, WIDTH), BF), pltpu.SemaphoreType.DMA((3,))],
        compiler_params=params(),
        name="final",
    )(dest.reshape(ROWS, 1), base, back)


def solution(mesh):
    fine = Mesh(mesh.devices.reshape(CHIPS, 2, 4, 4), ("z", "core", "y", "x"))
    group = ("z", "core")
    tensor = ("y", "x")
    in_specs = (
        P(group, tensor),
        P(None, tensor),
        P(group, None, tensor),
        P(group, None, tensor),
        P(group),
        P(),
    )
    return jax.shard_map(
        body, mesh=fine, in_specs=in_specs, out_specs=P(group, tensor), check_vma=False
    )
```
